512 devices in a mesh: group: 16 (over y, core), node: 32 (over x, z).
Axes of the slice: x: 4, y: 8, z: 8, core: 2. Of those that a mesh axis runs over, the one named last changes fastest.
Arguments:
- desc: bfloat16 [524288, 512], P(('group', 'node')), may hold values from -8 to 8
- scales: float32 [4, 524288], P(None, ('group', 'node')), may hold values from 0.5 to 2
- labels: int32 [524288], P(('group', 'node')), may hold values from -1000 to 999
- prior: bfloat16 [524288, 1000], P(('group', 'node')), may hold values from -6 to 6
- block_cols: int32 [4096, 2], P(('group', 'node')), may hold values from 0 to 255, as said below
- cross_group: int32 [65536, 1], P(('group', 'node')), may hold values from 0 to 15; in each aligned block of 128 rows (0 to 127, 128 to 255, ...) at most 12 rows name the same one
- cross_row: int32 [65536], P(('group', 'node')), may hold values from 0 to 1023
Outputs:
- scores: bfloat16 [524288, 1000], P(('group', 'node'))
The draws below stay inside these ranges and needn't reach their ends.
Inputs may be any that keep to these rules, and one draw needn't show every extreme that they name: `block_cols`: block row r of the device at node position p names tiles p * 8 to p * 8 + 8 of its group, the last being the next device's first tile, which the device at the last position never names. A device's first block row names its own first tile first; its last block row names the next device's first tile second, or at the last position its own last tile. `cross_group`: among the 128 cross entries of one device, at most 12 name any one group.
All inputs are finite; a program needn't handle non-finite values.
Results may differ from the reference program's by a relative error of at most 0.0039.
Values may be sent and summed in bfloat16 or wider, within the bound.
No kernel may reach another device: no remote copies, remote signals or barrier semaphores. Data moves between devices by JAX's collectives and lax.ppermute only.
A program may use at most 64 MiB of HBM per device.

```python
import math
import jax
import jax.numpy as jnp
import numpy as np
from jax import lax

D = 512
C = 1000
SCALE_BLK = 128
BLK = 128
R_DEV = 8
NODE_DEV = 1024
NODES = 524288
TILES = 4096
XROWS = 65536
CAP = 12
N_GROUP = 16
N_NODE = 32
DEVICES = 512


prototype_count = 8


def draw_desc(key, part):
    protos = jax.random.normal(jax.random.fold_in(key, 11), (prototype_count, D), jnp.float32)
    pick = jax.random.randint(jax.random.fold_in(key, 12), (NODES,), 0, prototype_count)
    base = jnp.take(protos, pick, axis=0)
    noise = jax.random.normal(jax.random.fold_in(key, 13), (NODES, D), jnp.float32)
    value = 0.75 * base + 0.65 * noise
    return jnp.clip(value, -8.0, 8.0).astype(jnp.bfloat16)


def draw_block_cols(key, part):
    tile = jnp.arange(TILES, dtype=jnp.int32)
    device = tile // R_DEV
    place = device % N_NODE
    row = tile % R_DEV
    last = place == N_NODE - 1
    span = jnp.where(last, R_DEV, R_DEV + 1)
    raw = jax.random.randint(jax.random.fold_in(key, 21), (TILES, 2), 0, 1 << 20)
    pick = raw % span[:, None]
    first = jnp.where(row == 0, 0, pick[:, 0])
    second = jnp.where(row == R_DEV - 1, jnp.where(last, R_DEV - 1, R_DEV), pick[:, 1])
    return (jnp.stack([first, second], 1) + (place * R_DEV)[:, None]).astype(jnp.int32)


def set_ends(array, own_key, smallest, largest):
    spot = [jax.random.randint(jax.random.fold_in(own_key, axis), (), 0, length) for axis, length in enumerate(array.shape)]
    widest = array.shape.index(max(array.shape))
    neighbour = spot[:widest] + [(spot[widest] + 1) % array.shape[widest]] + spot[widest + 1:]
    return array.at[tuple(spot)].set(smallest).at[tuple(neighbour)].set(largest)


def shard_levels(own_key, shape, split, smallest, high):
    factor_of, own = 1.0, jax.random.fold_in(own_key, 6)
    for dim, parts in split:
        draws = jnp.exp(jax.random.uniform(jax.random.fold_in(own, dim), (parts,), jnp.float32, smallest / len(split), high / len(split)))
        factor_of = factor_of * jnp.repeat(draws, shape[dim] // parts).reshape([-1 if axis == dim else 1 for axis in range(len(shape))])
    return factor_of


def deal_out(key, own, number, rows, count, top, most, skew):
    sequence = jax.random.permutation(key, count)
    packed, ordinary = shares(count, rows * top, most, skew, True), shares(count, rows * top, most, skew, False)
    places = jnp.arange(count)

    def named(tallies, turn):
        used = int((tallies > 0).sum())
        fixed = max(1, used // 4)
        passed = fixed + (places - fixed + turn * (used - fixed)) % max(1, count - fixed)
        return jnp.zeros((count,), jnp.int32).at[sequence[jnp.where(places < fixed, places, passed)]].set(jnp.asarray(tallies, jnp.int32))

    tallies = jnp.where(number % 4 == 0, named(packed, number // 4), named(ordinary, number - number // 4 - 1))
    mixed = jax.random.permutation(jax.random.fold_in(own, 3), count)
    giver, taker = mixed[0:count // 2 * 2:2], mixed[1:count // 2 * 2:2]
    slack = jnp.minimum(tallies[giver] - 1, most - tallies[taker]) // 2
    slack = jnp.where((giver == sequence[0]) | (taker == sequence[0]) | (tallies[taker] == 0), 0, jnp.maximum(slack, 0))
    passed = jax.random.randint(jax.random.fold_in(own, 4), (count // 2,), 0, 1 << 20) % (slack + 1)
    tallies = tallies.at[giver].add(-passed).at[taker].add(passed)
    members = jnp.searchsorted(jnp.cumsum(tallies), jnp.arange(rows * top), side="right").astype(jnp.int32)
    listing = members.reshape(top, rows).T
    listing = listing[jax.random.permutation(jax.random.fold_in(own, 1), rows)]
    turn = jax.random.randint(jax.random.fold_in(own, 2), (rows, 1), 0, top)
    return jnp.take_along_axis(listing, (jnp.arange(top)[None, :] + turn) % top, axis=1)


def shares(number_of, total, reach, lean, full):
    portions = [(1 << 20) // math.isqrt(standing ** lean) + 1 for standing in range(1, number_of + 1)]
    largest = reach if full else min(reach, max(-(-total // number_of), total * portions[0] // sum(portions)))
    least = 1 if total - largest >= number_of - 1 else 0
    given, spare = [largest] + [least] * (number_of - 1), total - largest - least * (number_of - 1)
    while spare > 0:
        free = [i for i in range(1, number_of) if given[i] < largest] or [i for i in range(1, number_of) if given[i] < reach]
        whole, left = sum([portions[i] for i in free]), spare
        for i in free:
            extra = min(reach - given[i], max(1, left * portions[i] // whole), spare)
            given[i] = given[i] + extra
            spare = spare - extra
    return np.array(given)


def centred(rng, shape, scale, limit, shards=(), held_as=jnp.bfloat16):
    result = jax.random.normal(rng, shape, jnp.float32) * scale
    if len(shards) > 0:
        result = shard_levels(rng, shape, shards, -0.22, 0.18) * result
    return jnp.clip(result, min=-limit, max=limit).astype(held_as)


def setup_inputs(seed: int = 0) -> dict:
    key_list = jax.random.split(jax.random.key(seed), 8)
    desc = draw_desc(jax.random.fold_in(key_list[7], 71), 0)
    scales = jnp.clip(jnp.exp(math.log(2.0) - 1.3862944 * jax.random.uniform(key_list[1], (D // SCALE_BLK, NODES), jnp.float32) ** shard_levels(key_list[1], (D // SCALE_BLK, NODES), ((1, 512),), -0.2, 0.2)), 0.5, 2.0)
    labels = set_ends(jax.random.randint(key_list[2], (NODES,), -C, C), jax.random.fold_in(key_list[2], 1), -C, C - 1).astype(jnp.int32)
    prior = centred(key_list[3], (NODES, C), 1.0, 6.0, ((0, 512),))
    block_cols = draw_block_cols(jax.random.fold_in(key_list[7], 71), 0)
    cross_group_keys = jax.random.split(jax.random.fold_in(key_list[5], 1), XROWS // BLK)
    cross_group_turns = jax.random.permutation(jax.random.fold_in(key_list[5], 3), XROWS // BLK)
    cross_group = jax.vmap(lambda own, number: deal_out(jax.random.fold_in(key_list[5], 2), own, number, BLK, N_GROUP, 1, CAP, 2))(cross_group_keys, cross_group_turns).reshape((XROWS, 1))
    cross_row = set_ends(jax.random.randint(key_list[6], (XROWS,), 0, NODE_DEV), jax.random.fold_in(key_list[6], 1), 0, NODE_DEV - 1).astype(jnp.int32)
    return dict(desc=desc, scales=scales, labels=labels, prior=prior, block_cols=block_cols, cross_group=cross_group, cross_row=cross_row)


alpha_mix = 0.8
eps_norm = 1e-06

def unit_rows(desc, scales):
    count = desc.shape[0]
    widened = desc.astype(jnp.float32).reshape(count, D // SCALE_BLK, SCALE_BLK)
    widened = widened * jnp.transpose(scales)[:, :, None]
    widened = widened.reshape(count, D)
    norm_inv = lax.rsqrt(lax.optimization_barrier(jnp.sum(widened * widened, axis=1, keepdims=True)) + eps_norm)
    return (widened * norm_inv).astype(jnp.bfloat16)

def affinities(own, picked, cross):
    near = jnp.einsum('rid,rkjd->rikj', own.astype(jnp.float32), picked.astype(jnp.float32))
    far = jnp.einsum('rid,jd->rij', own.astype(jnp.float32), cross.astype(jnp.float32))
    near = jnp.maximum(near, 0.0) ** 3
    far = jnp.maximum(far, 0.0) ** 3
    degree = lax.optimization_barrier(jnp.sum(near, axis=(2, 3))) + lax.optimization_barrier(jnp.sum(far, axis=2))
    return (near.astype(jnp.bfloat16), far.astype(jnp.bfloat16), lax.rsqrt(degree))

def spread(near_w, far_w, picked, cross):
    total = jnp.einsum('rikj,rkjc->ric', near_w.astype(jnp.float32), picked.astype(jnp.float32))
    return total + jnp.einsum('rij,jc->ric', far_w.astype(jnp.float32), cross.astype(jnp.float32))

def reference(desc, scales, labels, prior, block_cols, cross_group, cross_row):
    units = unit_rows(desc, scales)
    classes = jnp.arange(C, dtype=jnp.int32)
    seeds = jnp.where(labels[:, None] >= 0, (labels[:, None] == classes[None, :]).astype(jnp.bfloat16), prior)
    devices_all = jnp.arange(DEVICES, dtype=jnp.int32)

    def pieces(table, dev):
        place = dev % N_NODE
        width = table.shape[1]
        own = lax.dynamic_slice_in_dim(table, (dev * NODE_DEV).astype(jnp.int32), NODE_DEV, 0)
        after = jnp.minimum(dev + 1, DEVICES - 1).astype(jnp.int32)
        following = lax.dynamic_slice_in_dim(table, (after * NODE_DEV).astype(jnp.int32), BLK, 0)
        following = jnp.where(place < N_NODE - 1, following, jnp.zeros_like(following))
        extended = jnp.concatenate([own, following], 0).reshape(R_DEV + 1, BLK, width)
        target = lax.dynamic_slice_in_dim(cross_group[:, 0], (dev * BLK).astype(jnp.int32), BLK, 0)
        source = lax.dynamic_slice_in_dim(cross_row, (dev * BLK).astype(jnp.int32), BLK, 0)
        global_rows = ((target * N_NODE + place) * NODE_DEV + source).astype(jnp.int32)
        cross = jnp.take(table, global_rows, axis=0)
        return (own.reshape(R_DEV, BLK, width), extended, cross)

    def local_cols(dev):
        place = dev % N_NODE
        named = lax.dynamic_slice_in_dim(block_cols, (dev * R_DEV).astype(jnp.int32), R_DEV, 0) - place * R_DEV
        return jnp.concatenate([jnp.arange(R_DEV, dtype=jnp.int32)[:, None], named.astype(jnp.int32)], 1)

    def build(dev):
        own, extended, cross = pieces(units, dev)
        return affinities(own, extended[local_cols(dev)], cross)
    near_all, far_all, rinv_all = lax.map(build, devices_all)
    first = (rinv_all.reshape(NODES)[:, None] * seeds.astype(jnp.float32)).astype(jnp.bfloat16)

    def advance(current, last):

        def one(dev):
            own, extended, cross = pieces(current, dev)
            total = spread(near_all[dev], far_all[dev], extended[local_cols(dev)], cross)
            seed_rows = lax.dynamic_slice_in_dim(seeds, (dev * NODE_DEV).astype(jnp.int32), NODE_DEV, 0)
            seed_rows = seed_rows.reshape(R_DEV, BLK, C).astype(jnp.float32)
            weight = rinv_all[dev][:, :, None]
            mixed = alpha_mix * weight * total + (1.0 - alpha_mix) * seed_rows
            if last:
                return mixed.astype(jnp.bfloat16)
            return (weight * mixed).astype(jnp.bfloat16)
        return lax.map(one, devices_all).reshape(NODES, C)
    second = advance(first, False)
    return advance(second, True)
```

```python
import jax
import jax.numpy as jnp
from jax import lax
from jax.experimental import pallas as pl
from jax.experimental.pallas import tpu as pltpu
from jax.sharding import PartitionSpec as P

D = 512
C = 1000
CP = 1024
BLK = 128
ROWS = 1024
TILES = ROWS // BLK
GROUPS = 16
EXT = ROWS + BLK

alpha_mix = 0.8
eps_norm = 1e-06

F32 = jnp.float32
BF16 = jnp.bfloat16
VM = pl.BlockSpec(memory_space=pltpu.VMEM)
SM = pl.BlockSpec(memory_space=pltpu.SMEM)
NN = (((1,), (0,)), ((), ()))
NT = (((1,), (1,)), ((), ()))
TN = (((0,), (0,)), ((), ()))


def dot(a, b, dims=NN):
    return lax.dot_general(a, b, dims, preferred_element_type=F32)


def iota(shape, dim):
    return lax.broadcasted_iota(jnp.int32, shape, dim)


def call(body, name, outs, ins, scratch=(), flops=10**9, nbytes=10**6):
    specs = [SM if s else VM for s in ins]
    return pl.pallas_call(
        body,
        name=name,
        out_shape=[jax.ShapeDtypeStruct(s, t) for s, t in outs],
        in_specs=specs,
        out_specs=[VM] * len(outs),
        scratch_shapes=list(scratch),
        cost_estimate=pl.CostEstimate(flops=flops, bytes_accessed=nbytes, transcendentals=0),
        compiler_params=pltpu.CompilerParams(vmem_limit_bytes=32 * 2**20),
    )


def index_body(group_ref, row_ref, wanted_ref, place_ref):
    target = group_ref[...]
    rows = row_ref[...]
    member = (iota((GROUPS, BLK), 0) == target).astype(F32)
    before = (iota((BLK, BLK), 0) < iota((BLK, BLK), 1)).astype(BF16)
    earlier = dot(member.astype(BF16), before)
    slot = jnp.sum(earlier * member, axis=0, keepdims=True).astype(jnp.int32)
    in_slot = (iota((BLK, BLK), 0) == slot).astype(BF16)
    high = (rows >> 5).astype(F32)
    low = (rows & 31).astype(F32)
    wanted = 32.0 * dot((member * high).astype(BF16), in_slot, NT)
    wanted = wanted + dot((member * low).astype(BF16), in_slot, NT)
    wanted_ref[:, 0, :] = wanted.astype(jnp.int32)
    place_ref[0:1, :] = target
    place_ref[1:2, :] = slot


def unit_body(desc_ref, scales_ref, unit_ref, head_ref):
    columns = jnp.transpose(jnp.concatenate([scales_ref[...], scales_ref[...]], axis=0))
    parts = []
    total = None
    for k in range(D // BLK):
        x = desc_ref[:, k * BLK : (k + 1) * BLK].astype(F32) * columns[:, k : k + 1]
        parts.append(x)
        square = x * x
        total = square if total is None else total + square
    inv = lax.rsqrt(jnp.sum(total, axis=1, keepdims=True) + eps_norm)
    for k in range(D // BLK):
        out = (parts[k] * inv).astype(BF16)
        unit_ref[:, k * BLK : (k + 1) * BLK] = out
        head_ref[:, k * BLK : (k + 1) * BLK] = out[:BLK]


def request_rows(asked_ref):
    asked = jnp.broadcast_to(asked_ref[...].astype(F32), (GROUPS, 8, BLK))
    lane, row = iota((GROUPS, 8, BLK), 2), iota((GROUPS, 8, BLK), 1)
    node = iota((GROUPS, 8, ROWS), 2).astype(F32)
    made = []
    for slot in (row, 8 + row % 4):
        column = jnp.sum(jnp.where(lane == slot, asked, 0.0), axis=2, keepdims=True)
        made.append(jnp.where(node == column, 1.0, 0.0).astype(BF16).reshape(BLK, ROWS))
    return jnp.concatenate(made, axis=0)


def pack_rows(res, chunks, send_ref):
    first = iota((BLK, BLK), 0) % 8 < 4

    def part(start, k):
        return res[start : start + BLK, k * BLK : (k + 1) * BLK]

    def put(at, upper, lower):
        both = jnp.concatenate(
            [upper.reshape(GROUPS, 8, BLK), lower.reshape(GROUPS, 8, BLK)], axis=1
        )
        send_ref[:, at : at + 16, :] = both.astype(BF16)

    for k in range(chunks // 2):
        put(16 * k, part(0, 2 * k), part(0, 2 * k + 1))
    for m in range(chunks // 4):
        upper = jnp.where(first, part(BLK, 4 * m), part(BLK, 4 * m + 1))
        lower = jnp.where(first, part(BLK, 4 * m + 2), part(BLK, 4 * m + 3))
        put(8 * chunks + 16 * m, upper, lower)


def placers(place_ref):
    target, slot = place_ref[0:1, :], place_ref[1:2, :]
    row = iota((2 * BLK, BLK), 0)
    low, high = [], []
    for h in range(2):
        at = jnp.where(slot < 8, target * 16 + slot + 8 * h, -1)
        low.append((row == at).astype(F32).astype(BF16))
    for q in range(4):
        at = jnp.where(slot >= 8, target * 16 + slot - 8 + 4 * q, -1)
        high.append((row == at).astype(F32).astype(BF16))
    return jnp.concatenate(low, axis=1), jnp.concatenate(high, axis=1)


def received(recv_ref, at):
    return recv_ref[:, at : at + 16, :].reshape(2 * BLK, BLK)


def gather_units_body(asked_ref, unit_ref, send_ref):
    res = dot(request_rows(asked_ref), unit_ref[...])
    pack_rows(res, D // BLK, send_ref)


def cube_pos(values):
    positive = jnp.maximum(values, 0.0)
    return positive * positive * positive


def near_body(named_ref, unit_ref, next_ref, w_ref, degree_ref, ext_ref):
    ext_ref[:ROWS, :] = unit_ref[...]
    ext_ref[ROWS:, :] = next_ref[...]
    for r in range(TILES):
        own = ext_ref[r * BLK : (r + 1) * BLK, :]
        sources = [own]
        for k in range(2):
            start = pl.multiple_of(named_ref[r, k] * BLK, BLK)
            sources.append(ext_ref[pl.ds(start, BLK), :])
        degree = None
        for k, source in enumerate(sources):
            w = cube_pos(dot(source, own, NT))
            part = jnp.sum(w, axis=0, keepdims=True)
            degree = part if degree is None else degree + part
            w_ref[r, k * BLK : (k + 1) * BLK, :] = w.astype(BF16)
        degree_ref[r : r + 1, :] = degree


def seed_body(labels_ref, prior_ref, seed_ref):
    labels = labels_ref[...]
    for k in range(CP // BLK):
        size = min(BLK, C - k * BLK)
        prior = prior_ref[k * BLK : k * BLK + size, :].astype(F32)
        classes = iota((size, ROWS), 0) + k * BLK
        hot = jnp.where(classes == labels, 1.0, 0.0)
        seed = jnp.where(labels >= 0, hot, prior)
        if size < BLK:
            seed = jnp.concatenate([seed, jnp.zeros((BLK - size, ROWS), F32)], axis=0)
        seed_ref[k * BLK : (k + 1) * BLK, :] = seed.astype(BF16)


def degree_body(
    recv_ref, place_ref, asked_ref, unit_ref, near_ref, seed_ref,
    w_ref, rinv_ref, first_ref, head_ref, send_ref, far_ref,
):
    low, high = placers(place_ref)
    for m in range(D // (4 * BLK)):
        deep = dot(high, received(recv_ref, 4 * D // BLK * 2 + 16 * m), TN)
        for j in range(2):
            flat = dot(low, received(recv_ref, 16 * (2 * m + j)), TN)
            for h in range(2):
                k = 4 * m + 2 * j + h
                part = flat[h * BLK : (h + 1) * BLK] + deep[(2 * j + h) * BLK :][:BLK]
                far_ref[:, k * BLK : (k + 1) * BLK] = part.astype(BF16)
    far = far_ref[...]
    for r in range(TILES):
        cols = slice(r * BLK, (r + 1) * BLK)
        w = cube_pos(dot(far, unit_ref[cols, :], NT))
        w_ref[:, cols] = w.astype(BF16)
        degree = near_ref[r : r + 1, :] + jnp.sum(w, axis=0, keepdims=True)
        rinv = lax.rsqrt(degree)
        rinv_ref[0:1, cols] = rinv
        first_ref[:, cols] = (rinv * seed_ref[:, cols].astype(F32)).astype(BF16)
    head_ref[...] = first_ref[:, :BLK]
    pack_rows(dot(request_rows(asked_ref), first_ref[...], NT), CP // BLK, send_ref)


def spread_near_body(named_ref, own_ref, next_ref, w_ref, out_ref, ext_ref):
    ext_ref[:, :ROWS] = own_ref[...]
    ext_ref[:, ROWS:] = next_ref[...]
    for r in range(TILES):
        sources = [ext_ref[:, r * BLK : (r + 1) * BLK]]
        for k in range(2):
            start = pl.multiple_of(named_ref[r, k] * BLK, BLK)
            sources.append(ext_ref[:, pl.ds(start, BLK)])
        out_ref[:, r * BLK : (r + 1) * BLK] = dot(jnp.concatenate(sources, axis=1), w_ref[r])


def far_scores(recv_ref, place_ref, far_ref):
    low, high = placers(place_ref)
    for m in range(CP // (4 * BLK)):
        deep = dot(received(recv_ref, 8 * CP // BLK + 16 * m), high, TN)
        for j in range(2):
            flat = dot(received(recv_ref, 16 * (2 * m + j)), low, TN)
            for h in range(2):
                k = 4 * m + 2 * j + h
                part = flat[:, h * BLK : (h + 1) * BLK]
                part = part + deep[:, (2 * j + h) * BLK : (2 * j + h + 1) * BLK]
                far_ref[k * BLK : (k + 1) * BLK, :] = part.astype(BF16)


def second_body(
    recv_ref, place_ref, asked_ref, w_ref, near_ref, rinv_ref, seed_ref,
    second_ref, head_ref, send_ref, far_ref,
):
    far_scores(recv_ref, place_ref, far_ref)
    for r in range(TILES // 2):
        cols = slice(2 * r * BLK, 2 * (r + 1) * BLK)
        total = dot(far_ref[...], w_ref[:, cols]) + near_ref[:, cols]
        weight = rinv_ref[0:1, cols]
        mixed = (alpha_mix * weight) * total + (1.0 - alpha_mix) * seed_ref[:, cols].astype(F32)
        second_ref[:, cols] = (weight * mixed).astype(BF16)
    head_ref[...] = second_ref[:, :BLK]
    pack_rows(dot(request_rows(asked_ref), second_ref[...], NT), CP // BLK, send_ref)


def last_body(recv_ref, place_ref, w_ref, near_ref, rinv_ref, seed_ref, out_ref, far_ref):
    far_scores(recv_ref, place_ref, far_ref)
    for r in range(TILES // 2):
        cols = slice(2 * r * BLK, 2 * (r + 1) * BLK)
        total = dot(far_ref[:C, :], w_ref[:, cols]) + near_ref[:C, cols]
        weight = rinv_ref[0:1, cols]
        mixed = (alpha_mix * weight) * total + (1.0 - alpha_mix) * seed_ref[:C, cols].astype(F32)
        out_ref[:, cols] = mixed.astype(BF16)


def passed_back(block):
    size = lax.axis_size("node")
    return lax.ppermute(block, "node", [(i, i - 1) for i in range(1, size)])


def exchanged(block):
    return lax.all_to_all(block, "group", split_axis=0, concat_axis=0, tiled=True)


def local(desc, scales, labels, prior, block_cols, cross_group, cross_row):
    named = block_cols - lax.axis_index("node") * TILES
    wanted, place = call(
        index_body,
        "index",
        [((GROUPS, 1, BLK), jnp.int32), ((8, BLK), jnp.int32)],
        [0, 0],
    )(cross_group.reshape(1, BLK), cross_row.reshape(1, BLK))
    asked = exchanged(wanted)
    units, head = call(
        unit_body, "units", [((ROWS, D), BF16), ((BLK, D), BF16)], [0, 0], nbytes=4 * 10**6
    )(desc, scales)
    next_units = passed_back(head)
    (send,) = call(
        gather_units_body, "gather_units", [((GROUPS, 48, BLK), BF16)], [0, 0]
    )(asked, units)
    far_units = exchanged(send)
    near_w, near_degree = call(
        near_body,
        "near",
        [((TILES, 3 * BLK, BLK), BF16), ((TILES, BLK), F32)],
        [1, 0, 0],
        [pltpu.VMEM((EXT, D), BF16)],
    )(named, units, next_units)
    (seeds,) = call(seed_body, "seeds", [((CP, ROWS), BF16)], [0, 0], nbytes=4 * 10**6)(
        labels.reshape(1, ROWS), jnp.transpose(prior)
    )
    class_rows = ((CP, ROWS), BF16)
    stepped = [class_rows, ((CP, BLK), BF16), ((GROUPS, 96, BLK), BF16)]
    far_w, rinv, first, head, send = call(
        degree_body,
        "degree",
        [((BLK, ROWS), BF16), ((1, ROWS), F32)] + stepped,
        [0] * 6,
        [pltpu.VMEM((BLK, D), BF16)],
    )(far_units, place, asked, units, near_degree, seeds)

    def near_part(scores, head, name):
        return call(
            spread_near_body,
            name,
            [((CP, ROWS), F32)],
            [1, 0, 0, 0],
            [pltpu.VMEM((CP, EXT), BF16)],
            flops=2 * 10**9,
        )(named, scores, passed_back(head), near_w)[0]

    far_scratch = [pltpu.VMEM((CP, BLK), BF16)]
    recv = exchanged(send)
    near = near_part(first, head, "near_first")
    second, head, send = call(second_body, "second", stepped, [0] * 7, far_scratch)(
        recv, place, asked, far_w, near, rinv, seeds
    )
    recv = exchanged(send)
    near = near_part(second, head, "near_second")
    (out,) = call(last_body, "last", [((C, ROWS), BF16)], [0] * 6, far_scratch)(
        recv, place, far_w, near, rinv, seeds
    )
    return jnp.transpose(out)


def solution(mesh):
    both = ("group", "node")
    in_specs = (P(both, None), P(None, both), P(both), P(both, None), P(both, None), P(both, None), P(both))
    return jax.shard_map(
        local, mesh=mesh, in_specs=in_specs, out_specs=P(both, None), check_vma=False
    )
```

```python
import jax
import jax.numpy as jnp
from jax import lax
from jax.experimental import pallas as pl
from jax.experimental.pallas import tpu as pltpu
from jax.sharding import PartitionSpec as P

D = 512
C = 1000
CP = 1024
BLK = 128
ROWS = 1024
TILES = ROWS // BLK
GROUPS = 16
EXT = ROWS + BLK
PAIR = 2 * BLK
PAIRS = ROWS // PAIR
UNIT_WIDE = 12 * D
SCORE_WIDE = 6 * ROWS
WEIGHT_DEEP = 16 * TILES

alpha_mix = 0.8
eps_norm = 1e-06

F32 = jnp.float32
BF16 = jnp.bfloat16
VM = pl.BlockSpec(memory_space=pltpu.VMEM)
SM = pl.BlockSpec(memory_space=pltpu.SMEM)
HB = pl.BlockSpec(memory_space=pltpu.HBM)
SPECS = {"v": VM, "s": SM, "h": HB}
NN = (((1,), (0,)), ((), ()))
NT = (((1,), (1,)), ((), ()))
TN = (((0,), (0,)), ((), ()))


def dot(a, b, dims=NN):
    return lax.dot_general(a, b, dims, preferred_element_type=F32)


def iota(shape, dim):
    return lax.broadcasted_iota(jnp.int32, shape, dim)


def call(body, name, outs, ins, out_kinds=None, scratch=(), flops=10**9, nbytes=10**6, limit=44):
    out_kinds = out_kinds or "v" * len(outs)
    return pl.pallas_call(
        body,
        name=name,
        out_shape=[jax.ShapeDtypeStruct(s, t) for s, t in outs],
        in_specs=[SPECS[k] for k in ins],
        out_specs=[SPECS[k] for k in out_kinds],
        scratch_shapes=list(scratch),
        cost_estimate=pl.CostEstimate(flops=flops, bytes_accessed=nbytes, transcendentals=0),
        compiler_params=pltpu.CompilerParams(vmem_limit_bytes=limit * 2**20),
    )


def started(copies):
    for copy in copies:
        copy.start()
    return copies


def fetched(source_ref, to_ref, sems):
    made = []
    for r in range(PAIRS):
        cols = pl.ds(r * PAIR, PAIR)
        made.append(pltpu.make_async_copy(source_ref.at[:, cols], to_ref.at[:, cols], sems.at[r]))
    return started(made)


def index_body(group_any, row_any, wanted_ref, place_ref, group_ref, row_ref, sems):
    copies = started(
        [
            pltpu.make_async_copy(group_any, group_ref, sems.at[0]),
            pltpu.make_async_copy(row_any, row_ref, sems.at[1]),
        ]
    )
    for copy in copies:
        copy.wait()
    target = group_ref[...]
    rows = row_ref[...]
    member = (iota((GROUPS, BLK), 0) == target).astype(F32)
    before = (iota((BLK, BLK), 0) < iota((BLK, BLK), 1)).astype(BF16)
    earlier = dot(member.astype(BF16), before)
    slot = jnp.sum(earlier * member, axis=0, keepdims=True).astype(jnp.int32)
    in_slot = (iota((BLK, BLK), 0) == slot).astype(BF16)
    high = (rows >> 5).astype(F32)
    low = (rows & 31).astype(F32)
    wanted = 32.0 * dot((member * high).astype(BF16), in_slot, NT)
    wanted = wanted + dot((member * low).astype(BF16), in_slot, NT)
    wanted_ref[:, 0, :] = wanted.astype(jnp.int32)
    place_ref[0:1, :] = target
    place_ref[1:2, :] = slot


def unit_body(desc_ref, scales_ref, unit_ref, head_ref):
    columns = jnp.transpose(jnp.concatenate([scales_ref[...], scales_ref[...]], axis=0))
    parts = []
    total = None
    for k in range(D // BLK):
        x = desc_ref[:, k * BLK : (k + 1) * BLK].astype(F32) * columns[:, k : k + 1]
        parts.append(x)
        square = x * x
        total = square if total is None else total + square
    inv = lax.rsqrt(jnp.sum(total, axis=1, keepdims=True) + eps_norm)
    for k in range(D // BLK):
        out = (parts[k] * inv).astype(BF16)
        unit_ref[:, k * BLK : (k + 1) * BLK] = out
        head_ref[:, k * BLK : (k + 1) * BLK] = out[:BLK]


def request_rows(asked_ref):
    asked = jnp.broadcast_to(asked_ref[...].astype(F32), (GROUPS, 8, BLK))
    lane, row = iota((GROUPS, 8, BLK), 2), iota((GROUPS, 8, BLK), 1)
    node = iota((GROUPS, 8, ROWS), 2).astype(F32)
    made = []
    for slot in (row, 8 + row % 4):
        column = jnp.sum(jnp.where(lane == slot, asked, 0.0), axis=2, keepdims=True)
        made.append(jnp.where(node == column, 1.0, 0.0).astype(BF16).reshape(BLK, ROWS))
    return jnp.concatenate(made, axis=0)


def pack_rows(res, chunks, send_ref):
    first = iota((BLK, BLK), 0) % 8 < 4

    def part(start, k):
        return res[start : start + BLK, k * BLK : (k + 1) * BLK]

    def put(at, upper, lower):
        both = jnp.concatenate(
            [upper.reshape(GROUPS, 8, BLK), lower.reshape(GROUPS, 8, BLK)], axis=1
        )
        send_ref[:, at : at + 16, :] = both.astype(BF16)

    for k in range(chunks // 2):
        put(16 * k, part(0, 2 * k), part(0, 2 * k + 1))
    for m in range(chunks // 4):
        upper = jnp.where(first, part(BLK, 4 * m), part(BLK, 4 * m + 1))
        lower = jnp.where(first, part(BLK, 4 * m + 2), part(BLK, 4 * m + 3))
        put(8 * chunks + 16 * m, upper, lower)


def placers(place_ref):
    target, slot = place_ref[0:1, :], place_ref[1:2, :]
    row = iota((2 * BLK, BLK), 0)
    low, high = [], []
    for h in range(2):
        at = jnp.where(slot < 8, target * 16 + slot + 8 * h, -1)
        low.append((row == at).astype(F32).astype(BF16))
    for q in range(4):
        at = jnp.where(slot >= 8, target * 16 + slot - 8 + 4 * q, -1)
        high.append((row == at).astype(F32).astype(BF16))
    return jnp.concatenate(low, axis=1), jnp.concatenate(high, axis=1)


def received(recv_ref, at):
    return recv_ref[:, at : at + 16, :].reshape(2 * BLK, BLK)


def gather_units_body(asked_ref, unit_ref, send_ref):
    pack_rows(dot(request_rows(asked_ref), unit_ref[...]), D // BLK, send_ref)


def cube_pos(values):
    positive = jnp.maximum(values, 0.0)
    return positive * positive * positive


def near_body(
    named_ref, unit_ref, next_ref, w_any, after_ref, degree_ref, unit_any, ext_ref, w_ref, sem, w_sem
):
    ext_ref[:ROWS, :] = unit_ref[...]
    ext_ref[ROWS:, :] = next_ref[...]
    kept = pltpu.make_async_copy(
        ext_ref.at[pl.ds(0, ROWS), :], unit_any.at[:, pl.ds(0, D)], sem
    )
    kept.start()
    for r in range(TILES):
        own = ext_ref[r * BLK : (r + 1) * BLK, :]
        w = cube_pos(dot(own, own, NT))
        degree = jnp.sum(w, axis=0, keepdims=True)
        w_ref[r, :BLK, :] = w.astype(BF16)
        after = jnp.zeros((BLK, BLK), F32)
        for k in range(2):
            tile = named_ref[r, k]
            start = pl.multiple_of(tile * BLK, BLK)
            w = cube_pos(dot(ext_ref[pl.ds(start, BLK), :], own, NT))
            degree = degree + jnp.sum(w, axis=0, keepdims=True)
            w = w.astype(BF16).astype(F32)
            inside = (tile < TILES).astype(F32)
            after = after + w * (1.0 - inside)
            w_ref[r, (k + 1) * BLK : (k + 2) * BLK, :] = (w * inside).astype(BF16)
        after_ref[:, r * BLK : (r + 1) * BLK] = after.astype(BF16)
        degree_ref[r : r + 1, :] = degree
    w_copy = pltpu.make_async_copy(w_ref, w_any.at[pl.ds(0, TILES)], w_sem)
    w_copy.start()
    kept.wait()
    w_copy.wait()


def seed_body(labels_ref, prior_ref, seed_any, seed_ref, sem):
    labels = labels_ref[...]
    for k in range(CP // BLK):
        size = min(BLK, C - k * BLK)
        prior = prior_ref[k * BLK : k * BLK + size, :].astype(F32)
        classes = iota((size, ROWS), 0) + k * BLK
        hot = jnp.where(classes == labels, 1.0, 0.0)
        seed = jnp.where(labels >= 0, hot, prior)
        if size < BLK:
            seed = jnp.concatenate([seed, jnp.zeros((BLK - size, ROWS), F32)], axis=0)
        seed_ref[k * BLK : (k + 1) * BLK, :] = seed.astype(BF16)
    copy = pltpu.make_async_copy(seed_ref, seed_any.at[:, pl.ds(0, ROWS)], sem)
    copy.start()
    copy.wait()


def degree_body(
    recv_ref, place_ref, asked_ref, unit_any, near_ref, after_ref, seed_any,
    w_ref, rinv_ref, head_ref, send_ref, far_ref, unit_ref, seed_ref, first_ref, sem, sems,
):
    copy = pltpu.make_async_copy(unit_any.at[:, pl.ds(0, D)], unit_ref, sem)
    copy.start()
    arriving = fetched(seed_any, seed_ref, sems)
    low, high = placers(place_ref)
    for m in range(D // (4 * BLK)):
        deep = dot(high, received(recv_ref, 8 * D // BLK + 16 * m), TN)
        for j in range(2):
            flat = dot(low, received(recv_ref, 16 * (2 * m + j)), TN)
            for h in range(2):
                k = 4 * m + 2 * j + h
                part = flat[h * BLK : (h + 1) * BLK] + deep[(2 * j + h) * BLK :][:BLK]
                far_ref[:, k * BLK : (k + 1) * BLK] = part.astype(BF16)
    far = far_ref[...]
    copy.wait()
    for r in range(TILES):
        cols = slice(r * BLK, (r + 1) * BLK)
        w = cube_pos(dot(far, unit_ref[cols, :], NT))
        w_ref[:BLK, cols] = w.astype(BF16)
        degree = near_ref[r : r + 1, :] + jnp.sum(w, axis=0, keepdims=True)
        rinv = lax.rsqrt(degree)
        rinv_ref[0:1, cols] = rinv
        if r % 2 == 0:
            arriving[r // 2].wait()
        first_ref[:, cols] = (rinv * seed_ref[:, cols].astype(F32)).astype(BF16)
    w_ref[BLK:, :] = after_ref[...]
    head_ref[...] = first_ref[:, :BLK]
    pack_rows(dot(request_rows(asked_ref), first_ref[...], NT), CP // BLK, send_ref)


def spread_near(named_ref, source_ref, w_ref, r):
    sources = [source_ref[:, r * BLK : (r + 1) * BLK]]
    for k in range(2):
        start = pl.multiple_of(lax.rem(named_ref[r, k], TILES) * BLK, BLK)
        sources.append(source_ref[:, pl.ds(start, BLK)])
    return dot(jnp.concatenate(sources, axis=1), w_ref[r])


def mixed_near(total, weight, seed):
    return (alpha_mix * weight) * total + (1.0 - alpha_mix) * seed.astype(F32)


def near_first_body(
    named_ref, seed_any, rinv_ref, w_any, out_ref, seed_ref, first_ref, w_ref, sems, w_sem
):
    w_copy = pltpu.make_async_copy(w_any.at[pl.ds(0, TILES)], w_ref, w_sem)
    w_copy.start()
    arriving = fetched(seed_any, seed_ref, sems)
    for r in range(PAIRS):
        arriving[r].wait()
        cols = slice(r * PAIR, (r + 1) * PAIR)
        first_ref[:, cols] = (rinv_ref[0:1, cols] * seed_ref[:, cols].astype(F32)).astype(BF16)
    w_copy.wait()
    for r in range(TILES):
        cols = slice(r * BLK, (r + 1) * BLK)
        weight = rinv_ref[0:1, cols]
        total = spread_near(named_ref, first_ref, w_ref, r)
        out_ref[:, cols] = (weight * mixed_near(total, weight, seed_ref[:, cols])).astype(BF16)


def near_second_body(
    named_ref, second_any, seed_any, rinv_ref, w_any, out_ref,
    seed_ref, second_ref, w_ref, sems, seed_sems, w_sem,
):
    arriving = started([pltpu.make_async_copy(w_any.at[pl.ds(0, TILES)], w_ref, w_sem)])
    arriving += fetched(second_any, second_ref, sems) + fetched(seed_any, seed_ref, seed_sems)
    for copy in arriving:
        copy.wait()
    for r in range(TILES):
        cols = slice(r * BLK, (r + 1) * BLK)
        total = spread_near(named_ref, second_ref, w_ref, r)
        out_ref[:, cols] = mixed_near(total, rinv_ref[0:1, cols], seed_ref[:, cols]).astype(BF16)


def far_scores(recv_ref, place_ref, next_ref, far_ref):
    low, high = placers(place_ref)
    for m in range(CP // (4 * BLK)):
        deep = dot(received(recv_ref, 8 * CP // BLK + 16 * m), high, TN)
        for j in range(2):
            flat = dot(received(recv_ref, 16 * (2 * m + j)), low, TN)
            for h in range(2):
                k = 4 * m + 2 * j + h
                part = flat[:, h * BLK : (h + 1) * BLK]
                part = part + deep[:, (2 * j + h) * BLK : (2 * j + h + 1) * BLK]
                far_ref[k * BLK : (k + 1) * BLK, :BLK] = part.astype(BF16)
    far_ref[:, BLK:] = next_ref[...]


def second_body(
    recv_ref, place_ref, asked_ref, next_ref, w_ref, near_ref, rinv_ref,
    second_any, head_ref, send_ref, far_ref, second_ref, sems,
):
    far_scores(recv_ref, place_ref, next_ref, far_ref)
    leaving = []
    for r in range(PAIRS):
        cols = slice(r * PAIR, (r + 1) * PAIR)
        total = dot(far_ref[...], w_ref[:, cols])
        weight = rinv_ref[0:1, cols]
        total = near_ref[:, cols].astype(F32) + (alpha_mix * weight * weight) * total
        second_ref[:, cols] = total.astype(BF16)
        at = pl.ds(r * PAIR, PAIR)
        leaving += started(
            [pltpu.make_async_copy(second_ref.at[:, at], second_any.at[:, at], sems.at[r])]
        )
    head_ref[...] = second_ref[:, :BLK]
    pack_rows(dot(request_rows(asked_ref), second_ref[...], NT), CP // BLK, send_ref)
    for copy in leaving:
        copy.wait()


def last_body(
    recv_ref, place_ref, next_ref, w_ref, near_ref, rinv_ref, out_any, far_ref, out_ref, sems
):
    far_scores(recv_ref, place_ref, next_ref, far_ref)
    leaving = []
    for r in range(PAIRS):
        cols = slice(r * PAIR, (r + 1) * PAIR)
        total = dot(far_ref[:C, :], w_ref[:, cols])
        total = near_ref[:C, cols].astype(F32) + (alpha_mix * rinv_ref[0:1, cols]) * total
        out_ref[:, cols] = total.astype(BF16)
        at = pl.ds(r * PAIR, PAIR)
        leaving += started(
            [pltpu.make_async_copy(out_ref.at[:, at], out_any.at[:, at], sems.at[r])]
        )
    for copy in leaving:
        copy.wait()


def passed_back(block):
    size = lax.axis_size("node")
    return lax.ppermute(block, "node", [(i, i - 1) for i in range(1, size)])


def exchanged(block):
    return lax.all_to_all(block, "group", split_axis=0, concat_axis=0, tiled=True)


def local(desc, scales, labels, prior, block_cols, cross_group, cross_row):
    named = block_cols - lax.axis_index("node") * TILES
    sem = pltpu.SemaphoreType.DMA
    sems = pltpu.SemaphoreType.DMA((PAIRS,))
    row_vector = pltpu.VMEM((1, BLK), jnp.int32)
    plane = pltpu.VMEM((CP, ROWS), BF16)
    far_scratch = pltpu.VMEM((CP, 2 * BLK), BF16)
    near_w_scratch = pltpu.VMEM((TILES, 3 * BLK, BLK), BF16)
    wanted, place = call(
        index_body,
        "index",
        [((GROUPS, 1, BLK), jnp.int32), ((8, BLK), jnp.int32)],
        "hh",
        scratch=[row_vector, row_vector, pltpu.SemaphoreType.DMA((2,))],
        limit=60,
    )(cross_group.reshape(1, BLK), cross_row.reshape(1, BLK))
    asked = exchanged(wanted)
    units, head = call(
        unit_body,
        "units",
        [((ROWS, D), BF16), ((BLK, D), BF16)],
        "vv",
        nbytes=4 * 10**6,
        limit=60,
    )(desc, scales)
    next_units = passed_back(head)
    (send,) = call(gather_units_body, "gather_units", [((GROUPS, 48, BLK), BF16)], "vv")(asked, units)
    far_units = exchanged(send)
    near_w, after_w, near_degree, unit_wide = call(
        near_body,
        "near",
        [
            ((WEIGHT_DEEP, 3 * BLK, BLK), BF16),
            ((BLK, ROWS), BF16),
            ((TILES, BLK), F32),
            ((ROWS, UNIT_WIDE), BF16),
        ],
        "svv",
        "hvvh",
        scratch=[pltpu.VMEM((EXT, D), BF16), near_w_scratch, sem, sem],
    )(named, units, next_units)
    scores_shape = ((CP, ROWS), BF16)
    wide_shape = ((CP, SCORE_WIDE), BF16)
    (seeds,) = call(
        seed_body, "seeds", [wide_shape], "vv", "h", scratch=[plane, sem], nbytes=4 * 10**6
    )(labels.reshape(1, ROWS), jnp.transpose(prior))
    head_send = [((CP, BLK), BF16), ((GROUPS, 96, BLK), BF16)]
    w, rinv, head, send = call(
        degree_body,
        "degree",
        [((2 * BLK, ROWS), BF16), ((1, ROWS), F32)] + head_send,
        "vvvhvvh",
        scratch=[
            pltpu.VMEM((BLK, D), BF16), pltpu.VMEM((ROWS, D), BF16), plane, plane, sem, sems
        ],
        limit=50,
    )(far_units, place, asked, unit_wide, near_degree, after_w, seeds)
    recv = exchanged(send)
    next_head = passed_back(head)
    (near,) = call(
        near_first_body,
        "near_first",
        [scores_shape],
        "shvh",
        scratch=[plane, plane, near_w_scratch, sems, sem],
        flops=2 * 10**9,
    )(named, seeds, rinv, near_w)
    second, head, send = call(
        second_body,
        "second",
        [wide_shape] + head_send,
        "vvvvvvv",
        "hvv",
        scratch=[far_scratch, plane, sems],
        limit=50,
    )(recv, place, asked, next_head, w, near, rinv)
    recv = exchanged(send)
    next_head = passed_back(head)
    (near,) = call(
        near_second_body,
        "near_second",
        [scores_shape],
        "shhvh",
        scratch=[plane, plane, near_w_scratch, sems, sems, sem],
        flops=2 * 10**9,
    )(named, second, seeds, rinv, near_w)
    (out,) = call(
        last_body,
        "last",
        [((C, ROWS), BF16)],
        "vvvvvv",
        "h",
        scratch=[far_scratch, pltpu.VMEM((C, ROWS), BF16), sems],
    )(recv, place, next_head, w, near, rinv)
    return jnp.transpose(out)


def solution(mesh):
    both = ("group", "node")
    in_specs = (P(both, None), P(None, both), P(both), P(both, None), P(both, None), P(both, None), P(both))
    return jax.shard_map(
        local, mesh=mesh, in_specs=in_specs, out_specs=P(both, None), check_vma=False
    )
```

```python
import jax
import jax.numpy as jnp
from jax import lax
from jax.experimental import pallas as pl
from jax.experimental.pallas import tpu as pltpu
from jax.sharding import PartitionSpec as P

D = 512
C = 1000
CP = 1024
BLK = 128
ROWS = 1024
TILES = ROWS // BLK
GROUPS = 16
EXT = ROWS + BLK
PAIR = 2 * BLK
PAIRS = ROWS // PAIR
SCORE_WIDE = 6 * ROWS
BASE_WIDE = 3 * ROWS
WEIGHT_DEEP = 16 * TILES
HALF = ROWS // 2

alpha_mix = 0.8
eps_norm = 1e-06

F32 = jnp.float32
BF16 = jnp.bfloat16
VM = pl.BlockSpec(memory_space=pltpu.VMEM)
SM = pl.BlockSpec(memory_space=pltpu.SMEM)
HB = pl.BlockSpec(memory_space=pltpu.HBM)
SPECS = {"v": VM, "s": SM, "h": HB}
NN = (((1,), (0,)), ((), ()))
NT = (((1,), (1,)), ((), ()))
TN = (((0,), (0,)), ((), ()))


def dot(a, b, dims=NN):
    return lax.dot_general(a, b, dims, preferred_element_type=F32)


def iota(shape, dim):
    return lax.broadcasted_iota(jnp.int32, shape, dim)


def call(body, name, outs, ins, out_kinds=None, scratch=(), flops=10**9, nbytes=10**6, limit=44):
    out_kinds = out_kinds or "v" * len(outs)
    return pl.pallas_call(
        body,
        name=name,
        out_shape=[jax.ShapeDtypeStruct(s, t) for s, t in outs],
        in_specs=[SPECS[k] for k in ins],
        out_specs=[SPECS[k] for k in out_kinds],
        scratch_shapes=list(scratch),
        cost_estimate=pl.CostEstimate(flops=flops, bytes_accessed=nbytes, transcendentals=0),
        compiler_params=pltpu.CompilerParams(vmem_limit_bytes=limit * 2**20),
    )


def started(copies):
    for copy in copies:
        copy.start()
    return copies


def moved(source_ref, to_ref, sems, pairs=range(PAIRS), source_at=0, to_at=0):
    made = []
    for r in pairs:
        source = source_ref.at[:, pl.ds(r * PAIR + source_at, PAIR)]
        to = to_ref.at[:, pl.ds(r * PAIR + to_at, PAIR)]
        made.append(pltpu.make_async_copy(source, to, sems.at[r]))
    return started(made)


def index_body(group_any, row_any, wanted_ref, place_ref, group_ref, row_ref, sems):
    copies = started(
        [
            pltpu.make_async_copy(group_any, group_ref, sems.at[0]),
            pltpu.make_async_copy(row_any, row_ref, sems.at[1]),
        ]
    )
    for copy in copies:
        copy.wait()
    target = group_ref[...]
    rows = row_ref[...]
    member = (iota((GROUPS, BLK), 0) == target).astype(F32)
    before = (iota((BLK, BLK), 0) < iota((BLK, BLK), 1)).astype(BF16)
    earlier = dot(member.astype(BF16), before)
    slot = jnp.sum(earlier * member, axis=0, keepdims=True).astype(jnp.int32)
    in_slot = (iota((BLK, BLK), 0) == slot).astype(BF16)
    high = (rows >> 5).astype(F32)
    low = (rows & 31).astype(F32)
    wanted = 32.0 * dot((member * high).astype(BF16), in_slot, NT)
    wanted = wanted + dot((member * low).astype(BF16), in_slot, NT)
    wanted_ref[:, 0, :] = wanted.astype(jnp.int32)
    place_ref[0:1, :] = target
    place_ref[1:2, :] = slot


def unit_body(desc_ref, scales_ref, unit_ref, head_ref):
    columns = jnp.transpose(jnp.concatenate([scales_ref[...], scales_ref[...]], axis=0))
    parts = []
    total = None
    for k in range(D // BLK):
        x = desc_ref[:, k * BLK : (k + 1) * BLK].astype(F32) * columns[:, k : k + 1]
        parts.append(x)
        square = x * x
        total = square if total is None else total + square
    inv = lax.rsqrt(jnp.sum(total, axis=1, keepdims=True) + eps_norm)
    for k in range(D // BLK):
        out = (parts[k] * inv).astype(BF16)
        unit_ref[:, k * BLK : (k + 1) * BLK] = out
        head_ref[:, k * BLK : (k + 1) * BLK] = out[:BLK]


def asked_columns(asked_ref, rows):
    asked = jnp.broadcast_to(asked_ref[...].astype(F32), (GROUPS, rows, BLK))
    lane, row = iota((GROUPS, rows, BLK), 2), iota((GROUPS, rows, BLK), 1)
    return [
        jnp.sum(jnp.where(lane == slot, asked, 0.0), axis=2, keepdims=True)
        for slot in (row % 8, 8 + row % 4)
    ]


def request_rows(asked_ref):
    node = iota((GROUPS, 8, ROWS), 2).astype(F32)
    made = []
    for column in asked_columns(asked_ref, 8):
        made.append(jnp.where(node == column, 1.0, 0.0).astype(BF16).reshape(BLK, ROWS))
    return jnp.concatenate(made, axis=0)


def pack_rows(res, chunks, send_ref):
    first = iota((BLK, BLK), 0) % 8 < 4

    def part(start, k):
        return res[start : start + BLK, k * BLK : (k + 1) * BLK]

    def put(at, upper, lower):
        both = jnp.concatenate(
            [upper.reshape(GROUPS, 8, BLK), lower.reshape(GROUPS, 8, BLK)], axis=1
        )
        send_ref[:, at : at + 16, :] = both.astype(BF16)

    for k in range(chunks // 2):
        put(16 * k, part(0, 2 * k), part(0, 2 * k + 1))
    for m in range(chunks // 4):
        upper = jnp.where(first, part(BLK, 4 * m), part(BLK, 4 * m + 1))
        lower = jnp.where(first, part(BLK, 4 * m + 2), part(BLK, 4 * m + 3))
        put(8 * chunks + 16 * m, upper, lower)


def placers(place_ref):
    target, slot = place_ref[0:1, :], place_ref[1:2, :]
    row = iota((2 * BLK, BLK), 0)
    low, high = [], []
    for h in range(2):
        at = jnp.where(slot < 8, target * 16 + slot + 8 * h, -1)
        low.append((row == at).astype(F32).astype(BF16))
    for q in range(4):
        at = jnp.where(slot >= 8, target * 16 + slot - 8 + 4 * q, -1)
        high.append((row == at).astype(F32).astype(BF16))
    return jnp.concatenate(low, axis=1), jnp.concatenate(high, axis=1)


def received(recv_ref, at):
    return recv_ref[:, at : at + 16, :].reshape(2 * BLK, BLK)


def gather_units_body(asked_ref, unit_ref, send_ref):
    pack_rows(dot(request_rows(asked_ref), unit_ref[...]), D // BLK, send_ref)


def cube_pos(values):
    positive = jnp.maximum(values, 0.0)
    return positive * positive * positive


def near_body(named_ref, unit_ref, next_ref, w_any, after_ref, degree_ref, ext_ref, w_ref, w_sem):
    ext_ref[:ROWS, :] = unit_ref[...]
    ext_ref[ROWS:, :] = next_ref[...]
    for r in range(TILES):
        own = ext_ref[r * BLK : (r + 1) * BLK, :]
        w = cube_pos(dot(own, own, NT))
        degree = jnp.sum(w, axis=0, keepdims=True)
        w_ref[r, :BLK, :] = w.astype(BF16)
        after = jnp.zeros((BLK, BLK), F32)
        for k in range(2):
            tile = named_ref[r, k]
            start = pl.multiple_of(tile * BLK, BLK)
            w = cube_pos(dot(ext_ref[pl.ds(start, BLK), :], own, NT))
            degree = degree + jnp.sum(w, axis=0, keepdims=True)
            w = w.astype(BF16).astype(F32)
            inside = (tile < TILES).astype(F32)
            after = after + w * (1.0 - inside)
            w_ref[r, (k + 1) * BLK : (k + 2) * BLK, :] = (w * inside).astype(BF16)
        after_ref[:, r * BLK : (r + 1) * BLK] = after.astype(BF16)
        degree_ref[r : r + 1, :] = degree
    w_copy = pltpu.make_async_copy(w_ref, w_any.at[pl.ds(0, TILES)], w_sem)
    w_copy.start()
    w_copy.wait()


def seed_body(labels_ref, prior_ref, seed_any, seed_ref, sem):
    labels = labels_ref[...]
    for k in range(CP // BLK):
        size = min(BLK, C - k * BLK)
        prior = prior_ref[k * BLK : k * BLK + size, :].astype(F32)
        classes = iota((size, ROWS), 0) + k * BLK
        hot = jnp.where(classes == labels, 1.0, 0.0)
        seed = jnp.where(labels >= 0, hot, prior)
        if size < BLK:
            seed = jnp.concatenate([seed, jnp.zeros((BLK - size, ROWS), F32)], axis=0)
        seed_ref[k * BLK : (k + 1) * BLK, :] = seed.astype(BF16)
    copy = pltpu.make_async_copy(seed_ref, seed_any.at[:, pl.ds(0, ROWS)], sem)
    copy.start()
    copy.wait()


def gather_seeds_body(asked_ref, seed_any, send_ref, head_ref, seed_ref, sems):
    arriving = moved(seed_any, seed_ref, sems)
    rows = request_rows(asked_ref)
    for copy in arriving:
        copy.wait()
    head_ref[...] = seed_ref[:, :BLK]
    pack_rows(dot(rows, seed_ref[...], NT), CP // BLK, send_ref)


def degree_body(
    recv_ref, place_ref, asked_ref, unit_ref, near_ref, after_ref, asked_seed_ref, seed_ref,
    w_ref, rinv_ref, head_ref, send_ref, far_ref,
):
    low, high = placers(place_ref)
    for m in range(D // (4 * BLK)):
        deep = dot(high, received(recv_ref, 8 * D // BLK + 16 * m), TN)
        for j in range(2):
            flat = dot(low, received(recv_ref, 16 * (2 * m + j)), TN)
            for h in range(2):
                k = 4 * m + 2 * j + h
                part = flat[h * BLK : (h + 1) * BLK] + deep[(2 * j + h) * BLK :][:BLK]
                far_ref[:, k * BLK : (k + 1) * BLK] = part.astype(BF16)
    far = far_ref[...]
    columns = asked_columns(asked_ref, 16)
    node = iota((GROUPS, 16, BLK), 2).astype(F32)
    found = [jnp.zeros((GROUPS, 16, BLK), F32) for _ in columns]
    for r in range(TILES):
        cols = slice(r * BLK, (r + 1) * BLK)
        w = cube_pos(dot(far, unit_ref[cols, :], NT))
        w_ref[:BLK, cols] = w.astype(BF16)
        degree = near_ref[r : r + 1, :] + jnp.sum(w, axis=0, keepdims=True)
        rinv = lax.rsqrt(degree)
        rinv_ref[0:1, cols] = rinv
        if r == 0:
            head_ref[...] = (rinv * seed_ref[...].astype(F32)).astype(BF16)
        spread = jnp.broadcast_to(rinv.reshape(1, 1, BLK), (GROUPS, 16, BLK))
        for k, column in enumerate(columns):
            found[k] = jnp.where(node + float(r * BLK) == column, spread, found[k])
    w_ref[BLK:, :] = after_ref[...]
    weights = [jnp.sum(values, axis=2, keepdims=True) for values in found]
    for k in range(6):
        part = asked_seed_ref[:, 16 * k : 16 * (k + 1), :].astype(F32)
        send_ref[:, 16 * k : 16 * (k + 1), :] = (weights[k // 4] * part).astype(BF16)


def spread_near(named_ref, source_ref, w_ref, r):
    sources = [source_ref[:, r * BLK : (r + 1) * BLK]]
    for k in range(2):
        start = pl.multiple_of(lax.rem(named_ref[r, k], TILES) * BLK, BLK)
        sources.append(source_ref[:, pl.ds(start, BLK)])
    return dot(jnp.concatenate(sources, axis=1), w_ref[r])


def mixed_near(total, weight, seed):
    return (alpha_mix * weight) * total + (1.0 - alpha_mix) * seed.astype(F32)


def near_first_body(
    named_ref, seed_any, rinv_ref, w_any, low_ref, high_any,
    seed_ref, first_ref, w_ref, high_ref, sems, w_sem, high_sem,
):
    w_copy = pltpu.make_async_copy(w_any.at[pl.ds(0, TILES)], w_ref, w_sem)
    w_copy.start()
    arriving = moved(seed_any, seed_ref, sems)
    for r in range(PAIRS):
        arriving[r].wait()
        cols = slice(r * PAIR, (r + 1) * PAIR)
        first_ref[:, cols] = (rinv_ref[0:1, cols] * seed_ref[:, cols].astype(F32)).astype(BF16)
    w_copy.wait()
    for r in reversed(range(TILES)):
        cols = slice(r * BLK, (r + 1) * BLK)
        weight = rinv_ref[0:1, cols]
        total = spread_near(named_ref, first_ref, w_ref, r)
        total = (weight * mixed_near(total, weight, seed_ref[:, cols])).astype(BF16)
        if r < TILES // 2:
            low_ref[:, cols] = total
        else:
            high_ref[:, r * BLK - HALF : (r + 1) * BLK - HALF] = total
        if r == TILES // 2:
            leaving = pltpu.make_async_copy(high_ref, high_any.at[:, pl.ds(0, HALF)], high_sem)
            leaving.start()
    leaving.wait()


def near_second_body(
    named_ref, second_any, seed_any, rinv_ref, w_any, low_ref, high_any,
    seed_ref, second_ref, w_ref, high_ref, sems, seed_sems, w_sem, high_sem,
):
    arriving = started([pltpu.make_async_copy(w_any.at[pl.ds(0, TILES)], w_ref, w_sem)])
    arriving += moved(second_any, second_ref, sems) + moved(seed_any, seed_ref, seed_sems)
    for copy in arriving:
        copy.wait()
    for r in reversed(range(TILES)):
        cols = slice(r * BLK, (r + 1) * BLK)
        total = spread_near(named_ref, second_ref, w_ref, r)
        total = mixed_near(total, rinv_ref[0:1, cols], seed_ref[:, cols])
        if r < TILES // 2:
            low_ref[:, cols] = total
        else:
            high_ref[:, r * BLK - HALF : (r + 1) * BLK - HALF] = total
        if r == TILES // 2:
            leaving = pltpu.make_async_copy(high_ref, high_any.at[:, pl.ds(0, HALF)], high_sem)
            leaving.start()
    leaving.wait()


def far_scores(recv_ref, place_ref, next_ref, far_ref):
    low, high = placers(place_ref)
    for m in range(CP // (4 * BLK)):
        deep = dot(received(recv_ref, 8 * CP // BLK + 16 * m), high, TN)
        for j in range(2):
            flat = dot(received(recv_ref, 16 * (2 * m + j)), low, TN)
            for h in range(2):
                k = 4 * m + 2 * j + h
                part = flat[:, h * BLK : (h + 1) * BLK]
                part = part + deep[:, (2 * j + h) * BLK : (2 * j + h + 1) * BLK]
                far_ref[k * BLK : (k + 1) * BLK, :BLK] = part.astype(BF16)
    far_ref[:, BLK:] = next_ref[...]


def second_body(
    recv_ref, place_ref, asked_ref, next_ref, w_ref, low_ref, high_any, rinv_ref,
    second_any, head_ref, send_ref, far_ref, high_ref, second_ref, high_sem, sems,
):
    arriving = pltpu.make_async_copy(high_any.at[:, pl.ds(0, HALF)], high_ref, high_sem)
    arriving.start()
    far_scores(recv_ref, place_ref, next_ref, far_ref)
    leaving = []
    for r in range(PAIRS):
        cols = slice(r * PAIR, (r + 1) * PAIR)
        total = dot(far_ref[...], w_ref[:, cols])
        weight = rinv_ref[0:1, cols]
        if r == PAIRS // 2:
            arriving.wait()
        if r < PAIRS // 2:
            base = low_ref[:, cols]
        else:
            base = high_ref[:, r * PAIR - HALF : (r + 1) * PAIR - HALF]
        total = base.astype(F32) + (alpha_mix * weight * weight) * total
        second_ref[:, cols] = total.astype(BF16)
        leaving += moved(second_ref, second_any, sems, [r])
    head_ref[...] = second_ref[:, :BLK]
    pack_rows(dot(request_rows(asked_ref), second_ref[...], NT), CP // BLK, send_ref)
    for copy in leaving:
        copy.wait()


def last_body(
    recv_ref, place_ref, next_ref, w_ref, low_ref, high_any, rinv_ref,
    out_any, far_ref, high_ref, out_ref, high_sem, sems,
):
    arriving = pltpu.make_async_copy(high_any.at[:, pl.ds(0, HALF)], high_ref, high_sem)
    arriving.start()
    far_scores(recv_ref, place_ref, next_ref, far_ref)
    leaving = []
    for r in range(PAIRS):
        cols = slice(r * PAIR, (r + 1) * PAIR)
        total = dot(far_ref[:C, :], w_ref[:, cols])
        if r == PAIRS // 2:
            arriving.wait()
        if r < PAIRS // 2:
            base = low_ref[:C, cols]
        else:
            base = high_ref[:C, r * PAIR - HALF : (r + 1) * PAIR - HALF]
        out_ref[:, cols] = (base + (alpha_mix * rinv_ref[0:1, cols]) * total).astype(BF16)
        leaving += moved(out_ref, out_any, sems, [r])
    for copy in leaving:
        copy.wait()


def passed_back(block):
    size = lax.axis_size("node")
    return lax.ppermute(block, "node", [(i, i - 1) for i in range(1, size)])


def exchanged(block):
    return lax.all_to_all(block, "group", split_axis=0, concat_axis=0, tiled=True)


def local(desc, scales, labels, prior, block_cols, cross_group, cross_row):
    named = block_cols - lax.axis_index("node") * TILES
    sem = pltpu.SemaphoreType.DMA
    sems = pltpu.SemaphoreType.DMA((PAIRS,))
    row_vector = pltpu.VMEM((1, BLK), jnp.int32)
    plane = pltpu.VMEM((CP, ROWS), BF16)
    far_scratch = pltpu.VMEM((CP, 2 * BLK), BF16)
    near_w_scratch = pltpu.VMEM((TILES, 3 * BLK, BLK), BF16)
    wanted, place = call(
        index_body,
        "index",
        [((GROUPS, 1, BLK), jnp.int32), ((8, BLK), jnp.int32)],
        "hh",
        scratch=[row_vector, row_vector, pltpu.SemaphoreType.DMA((2,))],
        limit=60,
    )(cross_group.reshape(1, BLK), cross_row.reshape(1, BLK))
    asked = exchanged(wanted)
    units, head = call(
        unit_body,
        "units",
        [((ROWS, D), BF16), ((BLK, D), BF16)],
        "vv",
        nbytes=4 * 10**6,
        limit=60,
    )(desc, scales)
    next_units = passed_back(head)
    (send,) = call(gather_units_body, "gather_units", [((GROUPS, 48, BLK), BF16)], "vv")(asked, units)
    far_units = exchanged(send)
    near_w, after_w, near_degree = call(
        near_body,
        "near",
        [((WEIGHT_DEEP, 3 * BLK, BLK), BF16), ((BLK, ROWS), BF16), ((TILES, BLK), F32)],
        "svv",
        "hvv",
        scratch=[pltpu.VMEM((EXT, D), BF16), near_w_scratch, sem],
    )(named, units, next_units)
    wide_shape = ((CP, SCORE_WIDE), BF16)
    (seeds,) = call(
        seed_body, "seeds", [wide_shape], "vv", "h", scratch=[plane, sem], nbytes=4 * 10**6
    )(labels.reshape(1, ROWS), jnp.transpose(prior))
    head_shape, send_shape = ((CP, BLK), BF16), ((GROUPS, 96, BLK), BF16)
    asked_seeds, seed_head = call(
        gather_seeds_body, "gather_seeds", [send_shape, head_shape], "vh", scratch=[plane, sems]
    )(asked, seeds)
    w, rinv, head, send = call(
        degree_body,
        "degree",
        [((2 * BLK, ROWS), BF16), ((1, ROWS), F32), head_shape, send_shape],
        "vvvvvvvv",
        scratch=[pltpu.VMEM((BLK, D), BF16)],
        limit=50,
    )(far_units, place, asked, units, near_degree, after_w, asked_seeds, seed_head)
    recv = exchanged(send)
    next_head = passed_back(head)
    low, high = call(
        near_first_body,
        "near_first",
        [((CP, HALF), BF16), wide_shape],
        "shvh",
        "vh",
        scratch=[plane, plane, near_w_scratch, pltpu.VMEM((CP, HALF), BF16), sems, sem, sem],
        flops=2 * 10**9,
    )(named, seeds, rinv, near_w)
    second, head, send = call(
        second_body,
        "second",
        [wide_shape, head_shape, send_shape],
        "vvvvvvhv",
        "hvv",
        scratch=[far_scratch, pltpu.VMEM((CP, HALF), BF16), plane, sem, sems],
        limit=50,
    )(recv, place, asked, next_head, w, low, high, rinv)
    recv = exchanged(send)
    next_head = passed_back(head)
    low, high = call(
        near_second_body,
        "near_second",
        [((CP, HALF), F32), ((CP, BASE_WIDE), F32)],
        "shhvh",
        "vh",
        scratch=[plane, plane, near_w_scratch, pltpu.VMEM((CP, HALF), F32), sems, sems, sem, sem],
        flops=2 * 10**9,
    )(named, second, seeds, rinv, near_w)
    (out,) = call(
        last_body,
        "last",
        [((C, ROWS), BF16)],
        "vvvvvhv",
        "h",
        scratch=[
            far_scratch, pltpu.VMEM((CP, HALF), F32), pltpu.VMEM((C, ROWS), BF16), sem, sems
        ],
    )(recv, place, next_head, w, low, high, rinv)
    return jnp.transpose(out)


def solution(mesh):
    both = ("group", "node")
    in_specs = (P(both, None), P(None, both), P(both), P(both, None), P(both, None), P(both, None), P(both))
    return jax.shard_map(
        local, mesh=mesh, in_specs=in_specs, out_specs=P(both, None), check_vma=False
    )
```

```python
import jax
import jax.numpy as jnp
from jax import lax
from jax.experimental import pallas as pl
from jax.experimental.pallas import tpu as pltpu
from jax.sharding import PartitionSpec as P

D = 512
C = 1000
CP = 1024
BLK = 128
ROWS = 1024
TILES = ROWS // BLK
GROUPS = 16
EXT = ROWS + BLK
PAIR = 2 * BLK
PAIRS = ROWS // PAIR
SCORE_DEEP = 24
BASE_DEEP = 12
WEIGHT_DEEP = 16 * TILES
HALF = ROWS // 2

alpha_mix = 0.8
eps_norm = 1e-06

F32 = jnp.float32
BF16 = jnp.bfloat16
VM = pl.BlockSpec(memory_space=pltpu.VMEM)
SM = pl.BlockSpec(memory_space=pltpu.SMEM)
HB = pl.BlockSpec(memory_space=pltpu.HBM)
SPECS = {"v": VM, "s": SM, "h": HB}
NN = (((1,), (0,)), ((), ()))
NT = (((1,), (1,)), ((), ()))
TN = (((0,), (0,)), ((), ()))


def dot(a, b, dims=NN):
    return lax.dot_general(a, b, dims, preferred_element_type=F32)


def iota(shape, dim):
    return lax.broadcasted_iota(jnp.int32, shape, dim)


def call(body, name, outs, ins, out_kinds=None, scratch=(), flops=10**9, nbytes=10**6, limit=44):
    out_kinds = out_kinds or "v" * len(outs)
    return pl.pallas_call(
        body,
        name=name,
        out_shape=[jax.ShapeDtypeStruct(s, t) for s, t in outs],
        in_specs=[SPECS[k] for k in ins],
        out_specs=[SPECS[k] for k in out_kinds],
        scratch_shapes=list(scratch),
        cost_estimate=pl.CostEstimate(flops=flops, bytes_accessed=nbytes, transcendentals=0),
        compiler_params=pltpu.CompilerParams(vmem_limit_bytes=limit * 2**20),
    )


def started(copies):
    for copy in copies:
        copy.start()
    return copies


def arriving_pairs(pairs_any, to_ref, sems, count=PAIRS):
    return started(
        [
            pltpu.make_async_copy(
                pairs_any.at[r], to_ref.at[:, pl.ds(r * PAIR, PAIR)], sems.at[r]
            )
            for r in range(count)
        ]
    )


def leaving_pair(from_ref, pairs_any, sems, r):
    return started(
        [
            pltpu.make_async_copy(
                from_ref.at[:, pl.ds(r * PAIR, PAIR)], pairs_any.at[r], sems.at[r]
            )
        ]
    )


def index_body(group_any, row_any, wanted_ref, place_ref, group_ref, row_ref, sems):
    copies = started(
        [
            pltpu.make_async_copy(group_any, group_ref, sems.at[0]),
            pltpu.make_async_copy(row_any, row_ref, sems.at[1]),
        ]
    )
    for copy in copies:
        copy.wait()
    target = group_ref[...]
    rows = row_ref[...]
    member = (iota((GROUPS, BLK), 0) == target).astype(F32)
    before = (iota((BLK, BLK), 0) < iota((BLK, BLK), 1)).astype(BF16)
    earlier = dot(member.astype(BF16), before)
    slot = jnp.sum(earlier * member, axis=0, keepdims=True).astype(jnp.int32)
    in_slot = (iota((BLK, BLK), 0) == slot).astype(BF16)
    high = (rows >> 5).astype(F32)
    low = (rows & 31).astype(F32)
    wanted = 32.0 * dot((member * high).astype(BF16), in_slot, NT)
    wanted = wanted + dot((member * low).astype(BF16), in_slot, NT)
    wanted_ref[:, 0, :] = wanted.astype(jnp.int32)
    place_ref[0:1, :] = target
    place_ref[1:2, :] = slot


def unit_body(desc_ref, scales_ref, unit_ref, head_ref):
    columns = jnp.transpose(jnp.concatenate([scales_ref[...], scales_ref[...]], axis=0))
    parts = []
    total = None
    for k in range(D // BLK):
        x = desc_ref[:, k * BLK : (k + 1) * BLK].astype(F32) * columns[:, k : k + 1]
        parts.append(x)
        square = x * x
        total = square if total is None else total + square
    inv = lax.rsqrt(jnp.sum(total, axis=1, keepdims=True) + eps_norm)
    for k in range(D // BLK):
        out = (parts[k] * inv).astype(BF16)
        unit_ref[:, k * BLK : (k + 1) * BLK] = out
        head_ref[:, k * BLK : (k + 1) * BLK] = out[:BLK]


def asked_columns(asked_ref, rows):
    asked = jnp.broadcast_to(asked_ref[...].astype(F32), (GROUPS, rows, BLK))
    lane, row = iota((GROUPS, rows, BLK), 2), iota((GROUPS, rows, BLK), 1)
    return [
        jnp.sum(jnp.where(lane == slot, asked, 0.0), axis=2, keepdims=True)
        for slot in (row % 8, 8 + row % 4)
    ]


def request_rows(asked_ref):
    node = iota((GROUPS, 8, ROWS), 2).astype(F32)
    made = []
    for column in asked_columns(asked_ref, 8):
        made.append(jnp.where(node == column, 1.0, 0.0).astype(BF16).reshape(BLK, ROWS))
    return jnp.concatenate(made, axis=0)


def pack_rows(res, chunks, send_ref):
    first = iota((BLK, BLK), 0) % 8 < 4

    def part(start, k):
        return res[start : start + BLK, k * BLK : (k + 1) * BLK]

    def put(at, upper, lower):
        both = jnp.concatenate(
            [upper.reshape(GROUPS, 8, BLK), lower.reshape(GROUPS, 8, BLK)], axis=1
        )
        send_ref[:, at : at + 16, :] = both.astype(BF16)

    for k in range(chunks // 2):
        put(16 * k, part(0, 2 * k), part(0, 2 * k + 1))
    for m in range(chunks // 4):
        upper = jnp.where(first, part(BLK, 4 * m), part(BLK, 4 * m + 1))
        lower = jnp.where(first, part(BLK, 4 * m + 2), part(BLK, 4 * m + 3))
        put(8 * chunks + 16 * m, upper, lower)


def placers(place_ref):
    target, slot = place_ref[0:1, :], place_ref[1:2, :]
    row = iota((2 * BLK, BLK), 0)
    low, high = [], []
    for h in range(2):
        at = jnp.where(slot < 8, target * 16 + slot + 8 * h, -1)
        low.append((row == at).astype(F32).astype(BF16))
    for q in range(4):
        at = jnp.where(slot >= 8, target * 16 + slot - 8 + 4 * q, -1)
        high.append((row == at).astype(F32).astype(BF16))
    return jnp.concatenate(low, axis=1), jnp.concatenate(high, axis=1)


def received(recv_ref, at):
    return recv_ref[:, at : at + 16, :].reshape(2 * BLK, BLK)


def gather_units_body(asked_ref, unit_ref, send_ref):
    pack_rows(dot(request_rows(asked_ref), unit_ref[...]), D // BLK, send_ref)


def cube_pos(values):
    positive = jnp.maximum(values, 0.0)
    return positive * positive * positive


def near_body(named_ref, unit_ref, next_ref, w_any, after_ref, degree_ref, ext_ref, w_ref, w_sem):
    ext_ref[:ROWS, :] = unit_ref[...]
    ext_ref[ROWS:, :] = next_ref[...]
    for r in range(TILES):
        own = ext_ref[r * BLK : (r + 1) * BLK, :]
        w = cube_pos(dot(own, own, NT))
        degree = jnp.sum(w, axis=0, keepdims=True)
        w_ref[r, :BLK, :] = w.astype(BF16)
        after = jnp.zeros((BLK, BLK), F32)
        for k in range(2):
            tile = named_ref[r, k]
            start = pl.multiple_of(tile * BLK, BLK)
            w = cube_pos(dot(ext_ref[pl.ds(start, BLK), :], own, NT))
            degree = degree + jnp.sum(w, axis=0, keepdims=True)
            w = w.astype(BF16).astype(F32)
            inside = (tile < TILES).astype(F32)
            after = after + w * (1.0 - inside)
            w_ref[r, (k + 1) * BLK : (k + 2) * BLK, :] = (w * inside).astype(BF16)
        after_ref[:, r * BLK : (r + 1) * BLK] = after.astype(BF16)
        degree_ref[r : r + 1, :] = degree
    w_copy = pltpu.make_async_copy(w_ref, w_any.at[pl.ds(0, TILES)], w_sem)
    w_copy.start()
    w_copy.wait()


def seed_body(labels_ref, prior_ref, seed_any, seed_ref, sems):
    labels = labels_ref[...]
    for k in range(CP // BLK):
        size = min(BLK, C - k * BLK)
        prior = prior_ref[k * BLK : k * BLK + size, :].astype(F32)
        classes = iota((size, ROWS), 0) + k * BLK
        hot = jnp.where(classes == labels, 1.0, 0.0)
        seed = jnp.where(labels >= 0, hot, prior)
        if size < BLK:
            seed = jnp.concatenate([seed, jnp.zeros((BLK - size, ROWS), F32)], axis=0)
        seed_ref[k * BLK : (k + 1) * BLK, :] = seed.astype(BF16)
    leaving = []
    for r in range(PAIRS):
        leaving += leaving_pair(seed_ref, seed_any, sems, r)
    for copy in leaving:
        copy.wait()


def gather_seeds_body(asked_ref, seed_any, send_ref, head_ref, seed_ref, sems):
    arriving = arriving_pairs(seed_any, seed_ref, sems)
    rows = request_rows(asked_ref)
    for copy in arriving:
        copy.wait()
    head_ref[...] = seed_ref[:, :BLK]
    pack_rows(dot(rows, seed_ref[...], NT), CP // BLK, send_ref)


def degree_body(
    recv_ref, place_ref, asked_ref, unit_ref, near_ref, after_ref, asked_seed_ref, seed_ref,
    w_ref, rinv_ref, head_ref, send_ref, far_ref,
):
    low, high = placers(place_ref)
    for m in range(D // (4 * BLK)):
        deep = dot(high, received(recv_ref, 8 * D // BLK + 16 * m), TN)
        for j in range(2):
            flat = dot(low, received(recv_ref, 16 * (2 * m + j)), TN)
            for h in range(2):
                k = 4 * m + 2 * j + h
                part = flat[h * BLK : (h + 1) * BLK] + deep[(2 * j + h) * BLK :][:BLK]
                far_ref[:, k * BLK : (k + 1) * BLK] = part.astype(BF16)
    far = far_ref[...]
    columns = asked_columns(asked_ref, 16)
    node = iota((GROUPS, 16, BLK), 2).astype(F32)
    found = [jnp.zeros((GROUPS, 16, BLK), F32) for _ in columns]
    for r in range(TILES):
        cols = slice(r * BLK, (r + 1) * BLK)
        w = cube_pos(dot(far, unit_ref[cols, :], NT))
        w_ref[:BLK, cols] = w.astype(BF16)
        degree = near_ref[r : r + 1, :] + jnp.sum(w, axis=0, keepdims=True)
        rinv = lax.rsqrt(degree)
        rinv_ref[0:1, cols] = rinv
        if r == 0:
            head_ref[...] = (rinv * seed_ref[...].astype(F32)).astype(BF16)
        spread = jnp.broadcast_to(rinv.reshape(1, 1, BLK), (GROUPS, 16, BLK))
        for k, column in enumerate(columns):
            found[k] = jnp.where(node + float(r * BLK) == column, spread, found[k])
    w_ref[BLK:, :] = after_ref[...]
    weights = [jnp.sum(values, axis=2, keepdims=True) for values in found]
    for k in range(6):
        part = asked_seed_ref[:, 16 * k : 16 * (k + 1), :].astype(F32)
        send_ref[:, 16 * k : 16 * (k + 1), :] = (weights[k // 4] * part).astype(BF16)


def spread_near(named_ref, source_ref, w_ref, r):
    sources = [source_ref[:, r * BLK : (r + 1) * BLK]]
    for k in range(2):
        start = pl.multiple_of(lax.rem(named_ref[r, k], TILES) * BLK, BLK)
        sources.append(source_ref[:, pl.ds(start, BLK)])
    return dot(jnp.concatenate(sources, axis=1), w_ref[r])


def mixed_near(total, weight, seed):
    return (alpha_mix * weight) * total + (1.0 - alpha_mix) * seed.astype(F32)


def near_first_body(
    named_ref, seed_any, rinv_ref, w_any, low_ref, high_any,
    seed_ref, first_ref, w_ref, high_ref, sems, w_sem, high_sems,
):
    w_copy = pltpu.make_async_copy(w_any.at[pl.ds(0, TILES)], w_ref, w_sem)
    w_copy.start()
    arriving = arriving_pairs(seed_any, seed_ref, sems)
    for r in range(PAIRS):
        arriving[r].wait()
        cols = slice(r * PAIR, (r + 1) * PAIR)
        first_ref[:, cols] = (rinv_ref[0:1, cols] * seed_ref[:, cols].astype(F32)).astype(BF16)
    w_copy.wait()
    leaving = []
    for r in reversed(range(TILES)):
        cols = slice(r * BLK, (r + 1) * BLK)
        weight = rinv_ref[0:1, cols]
        total = spread_near(named_ref, first_ref, w_ref, r)
        total = (weight * mixed_near(total, weight, seed_ref[:, cols])).astype(BF16)
        if r < TILES // 2:
            low_ref[:, cols] = total
        else:
            high_ref[:, r * BLK - HALF : (r + 1) * BLK - HALF] = total
        if r >= TILES // 2 and r % 2 == 0:
            leaving += leaving_pair(high_ref, high_any, high_sems, (r - TILES // 2) // 2)
    for copy in leaving:
        copy.wait()


def near_second_body(
    named_ref, second_any, seed_any, rinv_ref, w_any, low_ref, high_any,
    seed_ref, second_ref, w_ref, high_ref, sems, seed_sems, w_sem, high_sems,
):
    arriving = started([pltpu.make_async_copy(w_any.at[pl.ds(0, TILES)], w_ref, w_sem)])
    arriving += arriving_pairs(second_any, second_ref, sems)
    arriving += arriving_pairs(seed_any, seed_ref, seed_sems)
    for copy in arriving:
        copy.wait()
    leaving = []
    for r in reversed(range(TILES)):
        cols = slice(r * BLK, (r + 1) * BLK)
        total = spread_near(named_ref, second_ref, w_ref, r)
        total = mixed_near(total, rinv_ref[0:1, cols], seed_ref[:, cols])
        if r < TILES // 2:
            low_ref[:, cols] = total
        else:
            high_ref[:, r * BLK - HALF : (r + 1) * BLK - HALF] = total
        if r >= TILES // 2 and r % 2 == 0:
            leaving += leaving_pair(high_ref, high_any, high_sems, (r - TILES // 2) // 2)
    for copy in leaving:
        copy.wait()


def far_scores(recv_ref, place_ref, next_ref, far_ref):
    low, high = placers(place_ref)
    for m in range(CP // (4 * BLK)):
        deep = dot(received(recv_ref, 8 * CP // BLK + 16 * m), high, TN)
        for j in range(2):
            flat = dot(received(recv_ref, 16 * (2 * m + j)), low, TN)
            for h in range(2):
                k = 4 * m + 2 * j + h
                part = flat[:, h * BLK : (h + 1) * BLK]
                part = part + deep[:, (2 * j + h) * BLK : (2 * j + h + 1) * BLK]
                far_ref[k * BLK : (k + 1) * BLK, :BLK] = part.astype(BF16)
    far_ref[:, BLK:] = next_ref[...]


def second_body(
    recv_ref, place_ref, asked_ref, next_ref, w_ref, low_ref, high_any, rinv_ref,
    second_any, head_ref, send_ref, far_ref, high_ref, second_ref, high_sems, sems,
):
    arriving = arriving_pairs(high_any, high_ref, high_sems, PAIRS // 2)
    far_scores(recv_ref, place_ref, next_ref, far_ref)
    leaving = []
    for r in range(PAIRS):
        cols = slice(r * PAIR, (r + 1) * PAIR)
        total = dot(far_ref[...], w_ref[:, cols])
        weight = rinv_ref[0:1, cols]
        if r >= PAIRS // 2:
            arriving[r - PAIRS // 2].wait()
        if r < PAIRS // 2:
            base = low_ref[:, cols]
        else:
            base = high_ref[:, r * PAIR - HALF : (r + 1) * PAIR - HALF]
        total = base.astype(F32) + (alpha_mix * weight * weight) * total
        second_ref[:, cols] = total.astype(BF16)
        leaving += leaving_pair(second_ref, second_any, sems, r)
    head_ref[...] = second_ref[:, :BLK]
    pack_rows(dot(request_rows(asked_ref), second_ref[...], NT), CP // BLK, send_ref)
    for copy in leaving:
        copy.wait()


def last_body(
    recv_ref, place_ref, next_ref, w_ref, low_ref, high_any, rinv_ref,
    out_any, far_ref, high_ref, out_ref, high_sems, sems,
):
    arriving = arriving_pairs(high_any, high_ref, high_sems, PAIRS // 2)
    far_scores(recv_ref, place_ref, next_ref, far_ref)
    leaving = []
    for r in range(PAIRS):
        cols = slice(r * PAIR, (r + 1) * PAIR)
        total = dot(far_ref[:C, :], w_ref[:, cols])
        if r >= PAIRS // 2:
            arriving[r - PAIRS // 2].wait()
        if r < PAIRS // 2:
            base = low_ref[:C, cols]
        else:
            base = high_ref[:C, r * PAIR - HALF : (r + 1) * PAIR - HALF]
        out_ref[:, cols] = (base + (alpha_mix * rinv_ref[0:1, cols]) * total).astype(BF16)
        at = pl.ds(r * PAIR, PAIR)
        leaving += started(
            [pltpu.make_async_copy(out_ref.at[:, at], out_any.at[:, at], sems.at[r])]
        )
    for copy in leaving:
        copy.wait()


def passed_back(block):
    size = lax.axis_size("node")
    return lax.ppermute(block, "node", [(i, i - 1) for i in range(1, size)])


def exchanged(block):
    return lax.all_to_all(block, "group", split_axis=0, concat_axis=0, tiled=True)


def local(desc, scales, labels, prior, block_cols, cross_group, cross_row):
    named = block_cols - lax.axis_index("node") * TILES
    sem = pltpu.SemaphoreType.DMA
    sems = pltpu.SemaphoreType.DMA((PAIRS,))
    row_vector = pltpu.VMEM((1, BLK), jnp.int32)
    plane = pltpu.VMEM((CP, ROWS), BF16)
    far_scratch = pltpu.VMEM((CP, 2 * BLK), BF16)
    near_w_scratch = pltpu.VMEM((TILES, 3 * BLK, BLK), BF16)
    wanted, place = call(
        index_body,
        "index",
        [((GROUPS, 1, BLK), jnp.int32), ((8, BLK), jnp.int32)],
        "hh",
        scratch=[row_vector, row_vector, pltpu.SemaphoreType.DMA((2,))],
        limit=60,
    )(cross_group.reshape(1, BLK), cross_row.reshape(1, BLK))
    asked = exchanged(wanted)
    units, head = call(
        unit_body,
        "units",
        [((ROWS, D), BF16), ((BLK, D), BF16)],
        "vv",
        nbytes=4 * 10**6,
    )(desc, scales)
    next_units = passed_back(head)
    (send,) = call(gather_units_body, "gather_units", [((GROUPS, 48, BLK), BF16)], "vv")(asked, units)
    far_units = exchanged(send)
    near_w, after_w, near_degree = call(
        near_body,
        "near",
        [((WEIGHT_DEEP, 3 * BLK, BLK), BF16), ((BLK, ROWS), BF16), ((TILES, BLK), F32)],
        "svv",
        "hvv",
        scratch=[pltpu.VMEM((EXT, D), BF16), near_w_scratch, sem],
    )(named, units, next_units)
    wide_shape = ((SCORE_DEEP, CP, PAIR), BF16)
    (seeds,) = call(
        seed_body, "seeds", [wide_shape], "vv", "h", scratch=[plane, sems], nbytes=4 * 10**6
    )(labels.reshape(1, ROWS), jnp.transpose(prior))
    head_shape, send_shape = ((CP, BLK), BF16), ((GROUPS, 96, BLK), BF16)
    asked_seeds, seed_head = call(
        gather_seeds_body, "gather_seeds", [send_shape, head_shape], "vh", scratch=[plane, sems]
    )(asked, seeds)
    w, rinv, head, send = call(
        degree_body,
        "degree",
        [((2 * BLK, ROWS), BF16), ((1, ROWS), F32), head_shape, send_shape],
        "vvvvvvvv",
        scratch=[pltpu.VMEM((BLK, D), BF16)],
        limit=50,
    )(far_units, place, asked, units, near_degree, after_w, asked_seeds, seed_head)
    recv = exchanged(send)
    next_head = passed_back(head)
    low, high = call(
        near_first_body,
        "near_first",
        [((CP, HALF), BF16), wide_shape],
        "shvh",
        "vh",
        scratch=[plane, plane, near_w_scratch, pltpu.VMEM((CP, HALF), BF16), sems, sem, sems],
        flops=2 * 10**9,
    )(named, seeds, rinv, near_w)
    second, head, send = call(
        second_body,
        "second",
        [wide_shape, head_shape, send_shape],
        "vvvvvvhv",
        "hvv",
        scratch=[far_scratch, pltpu.VMEM((CP, HALF), BF16), plane, sems, sems],
        limit=50,
    )(recv, place, asked, next_head, w, low, high, rinv)
    recv = exchanged(send)
    next_head = passed_back(head)
    low, high = call(
        near_second_body,
        "near_second",
        [((CP, HALF), F32), ((BASE_DEEP, CP, PAIR), F32)],
        "shhvh",
        "vh",
        scratch=[plane, plane, near_w_scratch, pltpu.VMEM((CP, HALF), F32), sems, sems, sem, sems],
        flops=2 * 10**9,
    )(named, second, seeds, rinv, near_w)
    (out,) = call(
        last_body,
        "last",
        [((C, ROWS), BF16)],
        "vvvvvhv",
        "h",
        scratch=[
            far_scratch, pltpu.VMEM((CP, HALF), F32), pltpu.VMEM((C, ROWS), BF16), sems, sems
        ],
    )(recv, place, next_head, w, low, high, rinv)
    return jnp.transpose(out)


def solution(mesh):
    both = ("group", "node")
    in_specs = (P(both, None), P(None, both), P(both), P(both, None), P(both, None), P(both, None), P(both))
    return jax.shard_map(
        local, mesh=mesh, in_specs=in_specs, out_specs=P(both, None), check_vma=False
    )
```

```python
import jax
import jax.numpy as jnp
from jax import lax
from jax.experimental import pallas as pl
from jax.experimental.pallas import tpu as pltpu
from jax.sharding import PartitionSpec as P

D = 512
C = 1000
CP = 1024
BLK = 128
ROWS = 1024
TILES = ROWS // BLK
GROUPS = 16
EXT = ROWS + BLK
PAIR = 2 * BLK
PAIRS = ROWS // PAIR
SCORE_DEEP = 24
WEIGHT_DEEP = 16 * TILES

alpha_mix = 0.8
eps_norm = 1e-06

F32 = jnp.float32
BF16 = jnp.bfloat16
VM = pl.BlockSpec(memory_space=pltpu.VMEM)
SM = pl.BlockSpec(memory_space=pltpu.SMEM)
HB = pl.BlockSpec(memory_space=pltpu.HBM)
SPECS = {"v": VM, "s": SM, "h": HB}
NN = (((1,), (0,)), ((), ()))
NT = (((1,), (1,)), ((), ()))
TN = (((0,), (0,)), ((), ()))


def dot(a, b, dims=NN):
    return lax.dot_general(a, b, dims, preferred_element_type=F32)


def iota(shape, dim):
    return lax.broadcasted_iota(jnp.int32, shape, dim)


def call(body, name, outs, ins, out_kinds=None, scratch=(), flops=10**9, nbytes=10**6, limit=44):
    out_kinds = out_kinds or "v" * len(outs)
    return pl.pallas_call(
        body,
        name=name,
        out_shape=[jax.ShapeDtypeStruct(s, t) for s, t in outs],
        in_specs=[SPECS[k] for k in ins],
        out_specs=[SPECS[k] for k in out_kinds],
        scratch_shapes=list(scratch),
        cost_estimate=pl.CostEstimate(flops=flops, bytes_accessed=nbytes, transcendentals=0),
        compiler_params=pltpu.CompilerParams(vmem_limit_bytes=limit * 2**20),
    )


def started(copies):
    for copy in copies:
        copy.start()
    return copies


def arriving_pairs(pairs_any, to_ref, sems, count=PAIRS):
    return started(
        [
            pltpu.make_async_copy(
                pairs_any.at[r], to_ref.at[:, pl.ds(r * PAIR, PAIR)], sems.at[r]
            )
            for r in range(count)
        ]
    )


def leaving_pair(from_ref, pairs_any, sems, r):
    return started(
        [
            pltpu.make_async_copy(
                from_ref.at[:, pl.ds(r * PAIR, PAIR)], pairs_any.at[r], sems.at[r]
            )
        ]
    )


def index_body(group_any, row_any, wanted_ref, place_ref, group_ref, row_ref, sems):
    copies = started(
        [
            pltpu.make_async_copy(group_any, group_ref, sems.at[0]),
            pltpu.make_async_copy(row_any, row_ref, sems.at[1]),
        ]
    )
    for copy in copies:
        copy.wait()
    target = group_ref[...]
    rows = row_ref[...]
    member = (iota((GROUPS, BLK), 0) == target).astype(F32)
    before = (iota((BLK, BLK), 0) < iota((BLK, BLK), 1)).astype(BF16)
    earlier = dot(member.astype(BF16), before)
    slot = jnp.sum(earlier * member, axis=0, keepdims=True).astype(jnp.int32)
    in_slot = (iota((BLK, BLK), 0) == slot).astype(BF16)
    high = (rows >> 5).astype(F32)
    low = (rows & 31).astype(F32)
    wanted = 32.0 * dot((member * high).astype(BF16), in_slot, NT)
    wanted = wanted + dot((member * low).astype(BF16), in_slot, NT)
    wanted_ref[:, 0, :] = wanted.astype(jnp.int32)
    place_ref[0:1, :] = target
    place_ref[1:2, :] = slot


def unit_body(desc_ref, scales_ref, unit_ref, head_ref):
    columns = jnp.transpose(jnp.concatenate([scales_ref[...], scales_ref[...]], axis=0))
    parts = []
    total = None
    for k in range(D // BLK):
        x = desc_ref[:, k * BLK : (k + 1) * BLK].astype(F32) * columns[:, k : k + 1]
        parts.append(x)
        square = x * x
        total = square if total is None else total + square
    inv = lax.rsqrt(jnp.sum(total, axis=1, keepdims=True) + eps_norm)
    for k in range(D // BLK):
        out = (parts[k] * inv).astype(BF16)
        unit_ref[:, k * BLK : (k + 1) * BLK] = out
        head_ref[:, k * BLK : (k + 1) * BLK] = out[:BLK]


def asked_columns(asked_ref, rows):
    asked = jnp.broadcast_to(asked_ref[...].astype(F32), (GROUPS, rows, BLK))
    lane, row = iota((GROUPS, rows, BLK), 2), iota((GROUPS, rows, BLK), 1)
    return [
        jnp.sum(jnp.where(lane == slot, asked, 0.0), axis=2, keepdims=True)
        for slot in (row % 8, 8 + row % 4)
    ]


def request_rows(asked_ref):
    node = iota((GROUPS, 8, ROWS), 2).astype(F32)
    made = []
    for column in asked_columns(asked_ref, 8):
        made.append(jnp.where(node == column, 1.0, 0.0).astype(BF16).reshape(BLK, ROWS))
    return jnp.concatenate(made, axis=0)


def pack_rows(res, chunks, send_ref):
    first = iota((BLK, BLK), 0) % 8 < 4

    def part(start, k):
        return res[start : start + BLK, k * BLK : (k + 1) * BLK]

    def put(at, upper, lower):
        both = jnp.concatenate(
            [upper.reshape(GROUPS, 8, BLK), lower.reshape(GROUPS, 8, BLK)], axis=1
        )
        send_ref[:, at : at + 16, :] = both.astype(BF16)

    for k in range(chunks // 2):
        put(16 * k, part(0, 2 * k), part(0, 2 * k + 1))
    for m in range(chunks // 4):
        upper = jnp.where(first, part(BLK, 4 * m), part(BLK, 4 * m + 1))
        lower = jnp.where(first, part(BLK, 4 * m + 2), part(BLK, 4 * m + 3))
        put(8 * chunks + 16 * m, upper, lower)


def placers(place_ref):
    target, slot = place_ref[0:1, :], place_ref[1:2, :]
    row = iota((2 * BLK, BLK), 0)
    low, high = [], []
    for h in range(2):
        at = jnp.where(slot < 8, target * 16 + slot + 8 * h, -1)
        low.append((row == at).astype(F32).astype(BF16))
    for q in range(4):
        at = jnp.where(slot >= 8, target * 16 + slot - 8 + 4 * q, -1)
        high.append((row == at).astype(F32).astype(BF16))
    return jnp.concatenate(low, axis=1), jnp.concatenate(high, axis=1)


def received(recv_ref, at):
    return recv_ref[:, at : at + 16, :].reshape(2 * BLK, BLK)


def gather_units_body(asked_ref, unit_ref, send_ref):
    pack_rows(dot(request_rows(asked_ref), unit_ref[...]), D // BLK, send_ref)


def cube_pos(values):
    positive = jnp.maximum(values, 0.0)
    return positive * positive * positive


def near_body(named_ref, unit_ref, next_ref, w_any, after_ref, degree_ref, ext_ref, w_ref, w_sem):
    ext_ref[:ROWS, :] = unit_ref[...]
    ext_ref[ROWS:, :] = next_ref[...]
    for r in range(TILES):
        own = ext_ref[r * BLK : (r + 1) * BLK, :]
        w = cube_pos(dot(own, own, NT))
        degree = jnp.sum(w, axis=0, keepdims=True)
        w_ref[r, :BLK, :] = w.astype(BF16)
        after = jnp.zeros((BLK, BLK), F32)
        for k in range(2):
            tile = named_ref[r, k]
            start = pl.multiple_of(tile * BLK, BLK)
            w = cube_pos(dot(ext_ref[pl.ds(start, BLK), :], own, NT))
            degree = degree + jnp.sum(w, axis=0, keepdims=True)
            w = w.astype(BF16).astype(F32)
            inside = (tile < TILES).astype(F32)
            after = after + w * (1.0 - inside)
            w_ref[r, (k + 1) * BLK : (k + 2) * BLK, :] = (w * inside).astype(BF16)
        after_ref[:, r * BLK : (r + 1) * BLK] = after.astype(BF16)
        degree_ref[r : r + 1, :] = degree
    w_copy = pltpu.make_async_copy(w_ref, w_any.at[pl.ds(0, TILES)], w_sem)
    w_copy.start()
    w_copy.wait()


def seed_body(
    asked_ref, labels_ref, prior_any, send_ref, head_ref, seed_any,
    prior_ref, seed_ref, in_sems, sems,
):
    arriving = []
    for r in range(PAIRS):
        at = pl.ds(r * PAIR, PAIR)
        arriving += started(
            [pltpu.make_async_copy(prior_any.at[:, at], prior_ref.at[:, at], in_sems.at[r])]
        )
    rows = request_rows(asked_ref)
    seed_ref[CP - 32 :, :] = jnp.zeros((32, ROWS), BF16)
    leaving = []
    for r in range(PAIRS):
        cols = slice(r * PAIR, (r + 1) * PAIR)
        labels = labels_ref[:, cols]
        arriving[r].wait()
        hot = jnp.where(iota((C, PAIR), 0) == labels, 1.0, 0.0)
        seed = jnp.where(labels >= 0, hot, prior_ref[:, cols].astype(F32))
        seed_ref[:C, cols] = seed.astype(BF16)
        leaving += leaving_pair(seed_ref, seed_any, sems, r)
    head_ref[...] = seed_ref[:, :BLK]
    pack_rows(dot(rows, seed_ref[...], NT), CP // BLK, send_ref)
    for copy in leaving:
        copy.wait()


def degree_body(
    recv_ref, place_ref, asked_ref, unit_ref, near_ref, after_ref, asked_seed_ref, seed_ref,
    w_any, rinv_ref, head_ref, send_ref, far_ref, w_ref, w_sem,
):
    w_ref[BLK:, :] = after_ref[...]
    low, high = placers(place_ref)
    for m in range(D // (4 * BLK)):
        deep = dot(high, received(recv_ref, 8 * D // BLK + 16 * m), TN)
        for j in range(2):
            flat = dot(low, received(recv_ref, 16 * (2 * m + j)), TN)
            for h in range(2):
                k = 4 * m + 2 * j + h
                part = flat[h * BLK : (h + 1) * BLK] + deep[(2 * j + h) * BLK :][:BLK]
                far_ref[:, k * BLK : (k + 1) * BLK] = part.astype(BF16)
    far = far_ref[...]
    columns = asked_columns(asked_ref, 16)
    node = iota((GROUPS, 16, BLK), 2).astype(F32)
    found = [jnp.zeros((GROUPS, 16, BLK), F32) for _ in columns]
    for r in range(TILES):
        cols = slice(r * BLK, (r + 1) * BLK)
        w = cube_pos(dot(far, unit_ref[cols, :], NT))
        w_ref[:BLK, cols] = w.astype(BF16)
        degree = near_ref[r : r + 1, :] + jnp.sum(w, axis=0, keepdims=True)
        rinv = lax.rsqrt(degree)
        rinv_ref[0:1, cols] = rinv
        if r == 0:
            head_ref[...] = (rinv * seed_ref[...].astype(F32)).astype(BF16)
        spread = jnp.broadcast_to(rinv.reshape(1, 1, BLK), (GROUPS, 16, BLK))
        for k, column in enumerate(columns):
            found[k] = jnp.where(node + float(r * BLK) == column, spread, found[k])
    w_copy = pltpu.make_async_copy(w_ref, w_any.at[0], w_sem)
    w_copy.start()
    weights = [jnp.sum(values, axis=2, keepdims=True) for values in found]
    for k in range(6):
        part = asked_seed_ref[:, 16 * k : 16 * (k + 1), :].astype(F32)
        send_ref[:, 16 * k : 16 * (k + 1), :] = (weights[k // 4] * part).astype(BF16)
    w_copy.wait()


def spread_near(named_ref, source_ref, w_ref, r):
    sources = [source_ref[:, r * BLK : (r + 1) * BLK]]
    for k in range(2):
        start = pl.multiple_of(lax.rem(named_ref[r, k], TILES) * BLK, BLK)
        sources.append(source_ref[:, pl.ds(start, BLK)])
    return dot(jnp.concatenate(sources, axis=1), w_ref[r])


def mixed_near(total, weight, seed):
    return (alpha_mix * weight) * total + (1.0 - alpha_mix) * seed.astype(F32)


def near_first_body(named_ref, seed_any, rinv_ref, w_any, base_ref, seed_ref, first_ref, w_ref, sems, w_sem):
    w_copy = pltpu.make_async_copy(w_any.at[pl.ds(0, TILES)], w_ref, w_sem)
    w_copy.start()
    arriving = arriving_pairs(seed_any, seed_ref, sems)
    for r in range(PAIRS):
        arriving[r].wait()
        cols = slice(r * PAIR, (r + 1) * PAIR)
        first_ref[:, cols] = (rinv_ref[0:1, cols] * seed_ref[:, cols].astype(F32)).astype(BF16)
    w_copy.wait()
    for r in range(TILES):
        cols = slice(r * BLK, (r + 1) * BLK)
        weight = rinv_ref[0:1, cols]
        total = spread_near(named_ref, first_ref, w_ref, r)
        base_ref[:, cols] = (weight * mixed_near(total, weight, seed_ref[:, cols])).astype(BF16)


def near_second_body(
    named_ref, second_any, seed_any, rinv_ref, w_any, base_ref,
    second_ref, seed_ref, w_ref, sems, seed_sems, w_sem,
):
    arriving = arriving_pairs(second_any, second_ref, sems)
    arriving += started([pltpu.make_async_copy(w_any.at[pl.ds(0, TILES)], w_ref, w_sem)])
    seeds = arriving_pairs(seed_any, seed_ref, seed_sems)
    for copy in arriving:
        copy.wait()
    for r in range(TILES):
        cols = slice(r * BLK, (r + 1) * BLK)
        total = spread_near(named_ref, second_ref, w_ref, r)
        if r % 2 == 0:
            seeds[r // 2].wait()
        base_ref[:, cols] = mixed_near(total, rinv_ref[0:1, cols], seed_ref[:, cols]).astype(BF16)


def far_scores(recv_ref, place_ref, next_ref, far_ref):
    low, high = placers(place_ref)
    for m in range(CP // (4 * BLK)):
        deep = dot(received(recv_ref, 8 * CP // BLK + 16 * m), high, TN)
        for j in range(2):
            flat = dot(received(recv_ref, 16 * (2 * m + j)), low, TN)
            for h in range(2):
                k = 4 * m + 2 * j + h
                part = flat[:, h * BLK : (h + 1) * BLK]
                part = part + deep[:, (2 * j + h) * BLK : (2 * j + h + 1) * BLK]
                far_ref[k * BLK : (k + 1) * BLK, :BLK] = part.astype(BF16)
    far_ref[:, BLK:] = next_ref[...]


def second_body(
    recv_ref, place_ref, asked_ref, next_ref, w_any, base_ref, rinv_ref,
    second_any, head_ref, send_ref, far_ref, w_ref, second_ref, w_sem, sems,
):
    w_copy = pltpu.make_async_copy(w_any.at[0], w_ref, w_sem)
    w_copy.start()
    far_scores(recv_ref, place_ref, next_ref, far_ref)
    w_copy.wait()
    leaving = []
    for r in range(PAIRS):
        cols = slice(r * PAIR, (r + 1) * PAIR)
        total = dot(far_ref[...], w_ref[:, cols])
        weight = rinv_ref[0:1, cols]
        total = base_ref[:, cols].astype(F32) + (alpha_mix * weight * weight) * total
        second_ref[:, cols] = total.astype(BF16)
        leaving += leaving_pair(second_ref, second_any, sems, r)
    head_ref[...] = second_ref[:, :BLK]
    pack_rows(dot(request_rows(asked_ref), second_ref[...], NT), CP // BLK, send_ref)
    for copy in leaving:
        copy.wait()


def last_body(
    recv_ref, place_ref, next_ref, w_any, base_ref, rinv_ref,
    out_any, far_ref, w_ref, out_ref, w_sem, sems,
):
    w_copy = pltpu.make_async_copy(w_any.at[0], w_ref, w_sem)
    w_copy.start()
    far_scores(recv_ref, place_ref, next_ref, far_ref)
    w_copy.wait()
    leaving = []
    for r in range(PAIRS):
        cols = slice(r * PAIR, (r + 1) * PAIR)
        total = dot(far_ref[:C, :], w_ref[:, cols])
        total = base_ref[:C, cols].astype(F32) + (alpha_mix * rinv_ref[0:1, cols]) * total
        out_ref[:, cols] = total.astype(BF16)
        at = pl.ds(r * PAIR, PAIR)
        leaving += started(
            [pltpu.make_async_copy(out_ref.at[:, at], out_any.at[:, at], sems.at[r])]
        )
    for copy in leaving:
        copy.wait()


def passed_back(block):
    size = lax.axis_size("node")
    return lax.ppermute(block, "node", [(i, i - 1) for i in range(1, size)])


def exchanged(block):
    return lax.all_to_all(block, "group", split_axis=0, concat_axis=0, tiled=True)


def local(desc, scales, labels, prior, block_cols, cross_group, cross_row):
    named = block_cols - lax.axis_index("node") * TILES
    sem = pltpu.SemaphoreType.DMA
    sems = pltpu.SemaphoreType.DMA((PAIRS,))
    row_vector = pltpu.VMEM((1, BLK), jnp.int32)
    plane = pltpu.VMEM((CP, ROWS), BF16)
    far_scratch = pltpu.VMEM((CP, 2 * BLK), BF16)
    w_scratch = pltpu.VMEM((2 * BLK, ROWS), BF16)
    near_w_scratch = pltpu.VMEM((TILES, 3 * BLK, BLK), BF16)
    wanted, place = call(
        index_body,
        "index",
        [((GROUPS, 1, BLK), jnp.int32), ((8, BLK), jnp.int32)],
        "hh",
        scratch=[row_vector, row_vector, pltpu.SemaphoreType.DMA((2,))],
        limit=60,
    )(cross_group.reshape(1, BLK), cross_row.reshape(1, BLK))
    asked = exchanged(wanted)
    units, head = call(
        unit_body,
        "units",
        [((ROWS, D), BF16), ((BLK, D), BF16)],
        "vv",
        nbytes=4 * 10**6,
    )(desc, scales)
    next_units = passed_back(head)
    (send,) = call(gather_units_body, "gather_units", [((GROUPS, 48, BLK), BF16)], "vv")(asked, units)
    far_units = exchanged(send)
    near_w, after_w, near_degree = call(
        near_body,
        "near",
        [((WEIGHT_DEEP, 3 * BLK, BLK), BF16), ((BLK, ROWS), BF16), ((TILES, BLK), F32)],
        "svv",
        "hvv",
        scratch=[pltpu.VMEM((EXT, D), BF16), near_w_scratch, sem],
    )(named, units, next_units)
    wide_shape = ((SCORE_DEEP, CP, PAIR), BF16)
    head_shape, send_shape = ((CP, BLK), BF16), ((GROUPS, 96, BLK), BF16)
    asked_seeds, seed_head, seeds = call(
        seed_body,
        "seeds",
        [send_shape, head_shape, wide_shape],
        "vvh",
        "vvh",
        scratch=[pltpu.VMEM((C, ROWS), BF16), plane, sems, sems],
        flops=2 * 10**9,
        limit=53,
    )(asked, labels.reshape(1, ROWS), jnp.transpose(prior))
    w, rinv, head, send = call(
        degree_body,
        "degree",
        [((SCORE_DEEP, 2 * BLK, ROWS), BF16), ((1, ROWS), F32), head_shape, send_shape],
        "vvvvvvvv",
        "hvvv",
        scratch=[pltpu.VMEM((BLK, D), BF16), w_scratch, sem],
        limit=50,
    )(far_units, place, asked, units, near_degree, after_w, asked_seeds, seed_head)
    recv = exchanged(send)
    next_head = passed_back(head)
    scores_shape = ((CP, ROWS), BF16)
    (base,) = call(
        near_first_body,
        "near_first",
        [scores_shape],
        "shvh",
        scratch=[plane, plane, near_w_scratch, sems, sem],
        flops=2 * 10**9,
    )(named, seeds, rinv, near_w)
    second, head, send = call(
        second_body,
        "second",
        [wide_shape, head_shape, send_shape],
        "vvvvhvv",
        "hvv",
        scratch=[far_scratch, w_scratch, plane, sem, sems],
        limit=50,
    )(recv, place, asked, next_head, w, base, rinv)
    recv = exchanged(send)
    next_head = passed_back(head)
    (base,) = call(
        near_second_body,
        "near_second",
        [scores_shape],
        "shhvh",
        scratch=[plane, plane, near_w_scratch, sems, sems, sem],
        flops=2 * 10**9,
    )(named, second, seeds, rinv, near_w)
    (out,) = call(
        last_body,
        "last",
        [((C, ROWS), BF16)],
        "vvvhvv",
        "h",
        scratch=[far_scratch, w_scratch, pltpu.VMEM((C, ROWS), BF16), sem, sems],
    )(recv, place, next_head, w, base, rinv)
    return jnp.transpose(out)


def solution(mesh):
    both = ("group", "node")
    in_specs = (P(both, None), P(None, both), P(both), P(both, None), P(both, None), P(both, None), P(both))
    return jax.shard_map(
        local, mesh=mesh, in_specs=in_specs, out_specs=P(both, None), check_vma=False
    )
```

```python
import jax
import jax.numpy as jnp
from jax import lax
from jax.experimental import pallas as pl
from jax.experimental.pallas import tpu as pltpu
from jax.sharding import PartitionSpec as P

D = 512
C = 1000
CP = 1024
BLK = 128
ROWS = 1024
TILES = ROWS // BLK
GROUPS = 16
EXT = ROWS + BLK
PAIR = 2 * BLK
PAIRS = ROWS // PAIR
SCORE_DEEP = 24
LOW = ROWS - PAIR
WEIGHT_DEEP = 16 * TILES

alpha_mix = 0.8
eps_norm = 1e-06

F32 = jnp.float32
BF16 = jnp.bfloat16
VM = pl.BlockSpec(memory_space=pltpu.VMEM)
SM = pl.BlockSpec(memory_space=pltpu.SMEM)
HB = pl.BlockSpec(memory_space=pltpu.HBM)
SPECS = {"v": VM, "s": SM, "h": HB}
NN = (((1,), (0,)), ((), ()))
NT = (((1,), (1,)), ((), ()))
TN = (((0,), (0,)), ((), ()))


def dot(a, b, dims=NN):
    return lax.dot_general(a, b, dims, preferred_element_type=F32)


def iota(shape, dim):
    return lax.broadcasted_iota(jnp.int32, shape, dim)


def call(body, name, outs, ins, out_kinds=None, scratch=(), flops=10**9, nbytes=10**6, limit=44):
    out_kinds = out_kinds or "v" * len(outs)
    return pl.pallas_call(
        body,
        name=name,
        out_shape=[jax.ShapeDtypeStruct(s, t) for s, t in outs],
        in_specs=[SPECS[k] for k in ins],
        out_specs=[SPECS[k] for k in out_kinds],
        scratch_shapes=list(scratch),
        cost_estimate=pl.CostEstimate(flops=flops, bytes_accessed=nbytes, transcendentals=0),
        compiler_params=pltpu.CompilerParams(vmem_limit_bytes=limit * 2**20),
    )


def started(copies):
    for copy in copies:
        copy.start()
    return copies


def arriving_pairs(pairs_any, to_ref, sems, count=PAIRS):
    return started(
        [
            pltpu.make_async_copy(
                pairs_any.at[r], to_ref.at[:, pl.ds(r * PAIR, PAIR)], sems.at[r]
            )
            for r in range(count)
        ]
    )


def leaving_pair(from_ref, pairs_any, sems, r):
    return started(
        [
            pltpu.make_async_copy(
                from_ref.at[:, pl.ds(r * PAIR, PAIR)], pairs_any.at[r], sems.at[r]
            )
        ]
    )


def index_body(group_any, row_any, wanted_ref, place_ref, group_ref, row_ref, sems):
    copies = started(
        [
            pltpu.make_async_copy(group_any, group_ref, sems.at[0]),
            pltpu.make_async_copy(row_any, row_ref, sems.at[1]),
        ]
    )
    for copy in copies:
        copy.wait()
    target = group_ref[...]
    rows = row_ref[...]
    member = (iota((GROUPS, BLK), 0) == target).astype(F32)
    before = (iota((BLK, BLK), 0) < iota((BLK, BLK), 1)).astype(BF16)
    earlier = dot(member.astype(BF16), before)
    slot = jnp.sum(earlier * member, axis=0, keepdims=True).astype(jnp.int32)
    in_slot = (iota((BLK, BLK), 0) == slot).astype(BF16)
    high = (rows >> 5).astype(F32)
    low = (rows & 31).astype(F32)
    wanted = 32.0 * dot((member * high).astype(BF16), in_slot, NT)
    wanted = wanted + dot((member * low).astype(BF16), in_slot, NT)
    wanted_ref[:, 0, :] = wanted.astype(jnp.int32)
    place_ref[0:1, :] = target
    place_ref[1:2, :] = slot


def unit_body(desc_ref, scales_ref, unit_ref):
    columns = jnp.transpose(jnp.concatenate([scales_ref[...], scales_ref[...]], axis=0))
    parts = []
    total = None
    for k in range(D // BLK):
        x = desc_ref[:, k * BLK : (k + 1) * BLK].astype(F32) * columns[:, k : k + 1]
        parts.append(x)
        square = x * x
        total = square if total is None else total + square
    inv = lax.rsqrt(jnp.sum(total, axis=1, keepdims=True) + eps_norm)
    for k in range(D // BLK):
        unit_ref[:, k * BLK : (k + 1) * BLK] = (parts[k] * inv).astype(BF16)


def asked_columns(asked_ref, rows):
    asked = jnp.broadcast_to(asked_ref[...].astype(F32), (GROUPS, rows, BLK))
    lane, row = iota((GROUPS, rows, BLK), 2), iota((GROUPS, rows, BLK), 1)
    return [
        jnp.sum(jnp.where(lane == slot, asked, 0.0), axis=2, keepdims=True)
        for slot in (row % 8, 8 + row % 4)
    ]


def request_rows(asked_ref):
    node = iota((GROUPS, 8, ROWS), 2).astype(F32)
    made = []
    for column in asked_columns(asked_ref, 8):
        made.append(jnp.where(node == column, 1.0, 0.0).astype(BF16).reshape(BLK, ROWS))
    return jnp.concatenate(made, axis=0)


def pack_rows(res, chunks, send_ref):
    first = iota((BLK, BLK), 0) % 8 < 4

    def part(start, k):
        return res[start : start + BLK, k * BLK : (k + 1) * BLK]

    def put(at, upper, lower):
        both = jnp.concatenate(
            [upper.reshape(GROUPS, 8, BLK), lower.reshape(GROUPS, 8, BLK)], axis=1
        )
        send_ref[:, at : at + 16, :] = both.astype(BF16)

    for k in range(chunks // 2):
        put(16 * k, part(0, 2 * k), part(0, 2 * k + 1))
    for m in range(chunks // 4):
        upper = jnp.where(first, part(BLK, 4 * m), part(BLK, 4 * m + 1))
        lower = jnp.where(first, part(BLK, 4 * m + 2), part(BLK, 4 * m + 3))
        put(8 * chunks + 16 * m, upper, lower)


def placers(place_ref):
    target, slot = place_ref[0:1, :], place_ref[1:2, :]
    row = iota((2 * BLK, BLK), 0)
    low, high = [], []
    for h in range(2):
        at = jnp.where(slot < 8, target * 16 + slot + 8 * h, -1)
        low.append((row == at).astype(F32).astype(BF16))
    for q in range(4):
        at = jnp.where(slot >= 8, target * 16 + slot - 8 + 4 * q, -1)
        high.append((row == at).astype(F32).astype(BF16))
    return jnp.concatenate(low, axis=1), jnp.concatenate(high, axis=1)


def received(recv_ref, at):
    return recv_ref[:, at : at + 16, :].reshape(2 * BLK, BLK)


def gather_units_body(asked_ref, unit_ref, send_ref, head_ref):
    head_ref[...] = unit_ref[:BLK, :]
    pack_rows(dot(request_rows(asked_ref), unit_ref[...]), D // BLK, send_ref)


def cube_pos(values):
    positive = jnp.maximum(values, 0.0)
    return positive * positive * positive


def near_body(named_ref, unit_ref, next_ref, w_any, after_ref, degree_ref, ext_ref, w_ref, w_sem):
    ext_ref[:ROWS, :] = unit_ref[...]
    ext_ref[ROWS:, :] = next_ref[...]
    for r in range(TILES):
        own = ext_ref[r * BLK : (r + 1) * BLK, :]
        w = cube_pos(dot(own, own, NT))
        degree = jnp.sum(w, axis=0, keepdims=True)
        w_ref[r, :BLK, :] = w.astype(BF16)
        after = jnp.zeros((BLK, BLK), F32)
        for k in range(2):
            tile = named_ref[r, k]
            start = pl.multiple_of(tile * BLK, BLK)
            w = cube_pos(dot(ext_ref[pl.ds(start, BLK), :], own, NT))
            degree = degree + jnp.sum(w, axis=0, keepdims=True)
            w = w.astype(BF16).astype(F32)
            inside = (tile < TILES).astype(F32)
            after = after + w * (1.0 - inside)
            w_ref[r, (k + 1) * BLK : (k + 2) * BLK, :] = (w * inside).astype(BF16)
        after_ref[:, r * BLK : (r + 1) * BLK] = after.astype(BF16)
        degree_ref[r : r + 1, :] = degree
    w_copy = pltpu.make_async_copy(w_ref, w_any.at[pl.ds(0, TILES)], w_sem)
    w_copy.start()
    w_copy.wait()


def seed_body(
    asked_ref, labels_ref, prior_any, send_ref, head_ref, seed_any,
    prior_ref, seed_ref, in_sems, sems,
):
    arriving = []
    for r in range(PAIRS):
        at = pl.ds(r * PAIR, PAIR)
        arriving += started(
            [pltpu.make_async_copy(prior_any.at[:, at], prior_ref.at[:, at], in_sems.at[r])]
        )
    rows = request_rows(asked_ref)
    seed_ref[CP - 32 :, :] = jnp.zeros((32, ROWS), BF16)
    leaving = []
    for r in range(PAIRS):
        cols = slice(r * PAIR, (r + 1) * PAIR)
        labels = labels_ref[:, cols]
        arriving[r].wait()
        hot = jnp.where(iota((C, PAIR), 0) == labels, 1.0, 0.0)
        seed = jnp.where(labels >= 0, hot, prior_ref[:, cols].astype(F32))
        seed_ref[:C, cols] = seed.astype(BF16)
        leaving += leaving_pair(seed_ref, seed_any, sems, r)
    head_ref[...] = seed_ref[:, :BLK]
    pack_rows(dot(rows, seed_ref[...], NT), CP // BLK, send_ref)
    for copy in leaving:
        copy.wait()


def degree_body(
    recv_ref, place_ref, asked_ref, unit_ref, near_ref, after_ref, asked_seed_ref, seed_ref,
    w_ref, rinv_ref, head_ref, send_ref, far_ref,
):
    w_ref[BLK:, :] = after_ref[...]
    low, high = placers(place_ref)
    for m in range(D // (4 * BLK)):
        deep = dot(high, received(recv_ref, 8 * D // BLK + 16 * m), TN)
        for j in range(2):
            flat = dot(low, received(recv_ref, 16 * (2 * m + j)), TN)
            for h in range(2):
                k = 4 * m + 2 * j + h
                part = flat[h * BLK : (h + 1) * BLK] + deep[(2 * j + h) * BLK :][:BLK]
                far_ref[:, k * BLK : (k + 1) * BLK] = part.astype(BF16)
    far = far_ref[...]
    columns = asked_columns(asked_ref, 16)
    node = iota((GROUPS, 16, BLK), 2).astype(F32)
    found = [jnp.zeros((GROUPS, 16, BLK), F32) for _ in columns]
    for r in range(TILES):
        cols = slice(r * BLK, (r + 1) * BLK)
        w = cube_pos(dot(far, unit_ref[cols, :], NT))
        w_ref[:BLK, cols] = w.astype(BF16)
        degree = near_ref[r : r + 1, :] + jnp.sum(w, axis=0, keepdims=True)
        rinv = lax.rsqrt(degree)
        rinv_ref[0:1, cols] = rinv
        if r == 0:
            head_ref[...] = (rinv * seed_ref[...].astype(F32)).astype(BF16)
        spread = jnp.broadcast_to(rinv.reshape(1, 1, BLK), (GROUPS, 16, BLK))
        for k, column in enumerate(columns):
            found[k] = jnp.where(node + float(r * BLK) == column, spread, found[k])
    weights = [jnp.sum(values, axis=2, keepdims=True) for values in found]
    for k in range(6):
        part = asked_seed_ref[:, 16 * k : 16 * (k + 1), :].astype(F32)
        send_ref[:, 16 * k : 16 * (k + 1), :] = (weights[k // 4] * part).astype(BF16)


def spread_near(named_ref, source_ref, w_ref, r):
    sources = [source_ref[:, r * BLK : (r + 1) * BLK]]
    for k in range(2):
        start = pl.multiple_of(lax.rem(named_ref[r, k], TILES) * BLK, BLK)
        sources.append(source_ref[:, pl.ds(start, BLK)])
    return dot(jnp.concatenate(sources, axis=1), w_ref[r])


def mixed_near(total, weight, seed):
    return (alpha_mix * weight) * total + (1.0 - alpha_mix) * seed.astype(F32)


def put_base(total, r, low_ref, high_ref):
    if r * BLK < LOW:
        low_ref[:, r * BLK : (r + 1) * BLK] = total.astype(BF16)
    else:
        high_ref[:, r * BLK - LOW : (r + 1) * BLK - LOW] = total.astype(BF16)


def near_first_body(
    named_ref, seed_any, rinv_ref, w_any, low_ref, high_any,
    seed_ref, first_ref, w_ref, high_ref, sems, w_sem, high_sem,
):
    w_copy = pltpu.make_async_copy(w_any.at[pl.ds(0, TILES)], w_ref, w_sem)
    w_copy.start()
    arriving = arriving_pairs(seed_any, seed_ref, sems)
    for r in range(PAIRS):
        arriving[r].wait()
        cols = slice(r * PAIR, (r + 1) * PAIR)
        first_ref[:, cols] = (rinv_ref[0:1, cols] * seed_ref[:, cols].astype(F32)).astype(BF16)
    w_copy.wait()
    for r in range(TILES):
        cols = slice(r * BLK, (r + 1) * BLK)
        weight = rinv_ref[0:1, cols]
        total = spread_near(named_ref, first_ref, w_ref, r)
        put_base(weight * mixed_near(total, weight, seed_ref[:, cols]), r, low_ref, high_ref)
    copy = pltpu.make_async_copy(high_ref, high_any.at[0], high_sem)
    copy.start()
    copy.wait()


def near_second_body(
    named_ref, second_any, seed_any, rinv_ref, w_any, low_ref, high_any,
    second_ref, seed_ref, w_ref, high_ref, sems, seed_sems, w_sem, high_sem,
):
    arriving = arriving_pairs(second_any, second_ref, sems)
    arriving += started([pltpu.make_async_copy(w_any.at[pl.ds(0, TILES)], w_ref, w_sem)])
    seeds = arriving_pairs(seed_any, seed_ref, seed_sems)
    for copy in arriving:
        copy.wait()
    for r in range(TILES):
        cols = slice(r * BLK, (r + 1) * BLK)
        total = spread_near(named_ref, second_ref, w_ref, r)
        if r % 2 == 0:
            seeds[r // 2].wait()
        put_base(mixed_near(total, rinv_ref[0:1, cols], seed_ref[:, cols]), r, low_ref, high_ref)
    copy = pltpu.make_async_copy(high_ref, high_any.at[0], high_sem)
    copy.start()
    copy.wait()


def far_scores(recv_ref, place_ref, next_ref, far_ref):
    low, high = placers(place_ref)
    for m in range(CP // (4 * BLK)):
        deep = dot(received(recv_ref, 8 * CP // BLK + 16 * m), high, TN)
        for j in range(2):
            flat = dot(received(recv_ref, 16 * (2 * m + j)), low, TN)
            for h in range(2):
                k = 4 * m + 2 * j + h
                part = flat[:, h * BLK : (h + 1) * BLK]
                part = part + deep[:, (2 * j + h) * BLK : (2 * j + h + 1) * BLK]
                far_ref[k * BLK : (k + 1) * BLK, :BLK] = part.astype(BF16)
    far_ref[:, BLK:] = next_ref[...]


def second_body(
    recv_ref, place_ref, asked_ref, next_ref, w_ref, low_ref, high_any, rinv_ref,
    second_any, head_ref, send_ref, far_ref, high_ref, second_ref, high_sem, sems,
):
    arriving = pltpu.make_async_copy(high_any.at[0], high_ref, high_sem)
    arriving.start()
    far_scores(recv_ref, place_ref, next_ref, far_ref)
    leaving = []
    for r in range(PAIRS):
        cols = slice(r * PAIR, (r + 1) * PAIR)
        total = dot(far_ref[...], w_ref[:, cols])
        weight = rinv_ref[0:1, cols]
        if r == PAIRS - 1:
            arriving.wait()
        base = low_ref[:, cols] if r < PAIRS - 1 else high_ref[...]
        total = base.astype(F32) + (alpha_mix * weight * weight) * total
        second_ref[:, cols] = total.astype(BF16)
        leaving += leaving_pair(second_ref, second_any, sems, r)
    head_ref[...] = second_ref[:, :BLK]
    pack_rows(dot(request_rows(asked_ref), second_ref[...], NT), CP // BLK, send_ref)
    for copy in leaving:
        copy.wait()


def last_body(
    recv_ref, place_ref, next_ref, w_ref, low_ref, high_any, rinv_ref,
    out_any, far_ref, high_ref, out_ref, high_sem, sems,
):
    arriving = pltpu.make_async_copy(high_any.at[0], high_ref, high_sem)
    arriving.start()
    far_scores(recv_ref, place_ref, next_ref, far_ref)
    leaving = []
    for r in range(PAIRS):
        cols = slice(r * PAIR, (r + 1) * PAIR)
        total = dot(far_ref[:C, :], w_ref[:, cols])
        if r == PAIRS - 1:
            arriving.wait()
        base = low_ref[:C, cols] if r < PAIRS - 1 else high_ref[:C, :]
        total = base.astype(F32) + (alpha_mix * rinv_ref[0:1, cols]) * total
        out_ref[:, cols] = total.astype(BF16)
        at = pl.ds(r * PAIR, PAIR)
        leaving += started(
            [pltpu.make_async_copy(out_ref.at[:, at], out_any.at[:, at], sems.at[r])]
        )
    for copy in leaving:
        copy.wait()


def passed_back(block):
    size = lax.axis_size("node")
    return lax.ppermute(block, "node", [(i, i - 1) for i in range(1, size)])


def exchanged(block):
    return lax.all_to_all(block, "group", split_axis=0, concat_axis=0, tiled=True)


def local(desc, scales, labels, prior, block_cols, cross_group, cross_row):
    named = block_cols - lax.axis_index("node") * TILES
    sem = pltpu.SemaphoreType.DMA
    sems = pltpu.SemaphoreType.DMA((PAIRS,))
    row_vector = pltpu.VMEM((1, BLK), jnp.int32)
    plane = pltpu.VMEM((CP, ROWS), BF16)
    far_scratch = pltpu.VMEM((CP, 2 * BLK), BF16)
    last_pair = pltpu.VMEM((CP, PAIR), BF16)
    base_shapes = [((CP, LOW), BF16), ((SCORE_DEEP, CP, PAIR), BF16)]
    near_w_scratch = pltpu.VMEM((TILES, 3 * BLK, BLK), BF16)
    wanted, place = call(
        index_body,
        "index",
        [((GROUPS, 1, BLK), jnp.int32), ((8, BLK), jnp.int32)],
        "hh",
        scratch=[row_vector, row_vector, pltpu.SemaphoreType.DMA((2,))],
        limit=60,
    )(cross_group.reshape(1, BLK), cross_row.reshape(1, BLK))
    asked = exchanged(wanted)
    (units,) = call(unit_body, "units", [((ROWS, D), BF16)], "vv", nbytes=4 * 10**6)(desc, scales)
    send, head = call(
        gather_units_body,
        "gather_units",
        [((GROUPS, 48, BLK), BF16), ((BLK, D), BF16)],
        "vv",
    )(asked, units)
    far_units = exchanged(send)
    next_units = passed_back(head)
    near_w, after_w, near_degree = call(
        near_body,
        "near",
        [((WEIGHT_DEEP, 3 * BLK, BLK), BF16), ((BLK, ROWS), BF16), ((TILES, BLK), F32)],
        "svv",
        "hvv",
        scratch=[pltpu.VMEM((EXT, D), BF16), near_w_scratch, sem],
    )(named, units, next_units)
    wide_shape = ((SCORE_DEEP, CP, PAIR), BF16)
    head_shape, send_shape = ((CP, BLK), BF16), ((GROUPS, 96, BLK), BF16)
    asked_seeds, seed_head, seeds = call(
        seed_body,
        "seeds",
        [send_shape, head_shape, wide_shape],
        "vvh",
        "vvh",
        scratch=[pltpu.VMEM((C, ROWS), BF16), plane, sems, sems],
        flops=2 * 10**9,
        limit=53,
    )(asked, labels.reshape(1, ROWS), jnp.transpose(prior))
    w, rinv, head, send = call(
        degree_body,
        "degree",
        [((2 * BLK, ROWS), BF16), ((1, ROWS), F32), head_shape, send_shape],
        "vvvvvvvv",
        scratch=[pltpu.VMEM((BLK, D), BF16)],
        limit=50,
    )(far_units, place, asked, units, near_degree, after_w, asked_seeds, seed_head)
    recv = exchanged(send)
    next_head = passed_back(head)
    low, high = call(
        near_first_body,
        "near_first",
        base_shapes,
        "shvh",
        "vh",
        scratch=[plane, plane, near_w_scratch, last_pair, sems, sem, sem],
        flops=2 * 10**9,
    )(named, seeds, rinv, near_w)
    second, head, send = call(
        second_body,
        "second",
        [wide_shape, head_shape, send_shape],
        "vvvvvvhv",
        "hvv",
        scratch=[far_scratch, last_pair, plane, sem, sems],
        limit=50,
    )(recv, place, asked, next_head, w, low, high, rinv)
    recv = exchanged(send)
    next_head = passed_back(head)
    low, high = call(
        near_second_body,
        "near_second",
        base_shapes,
        "shhvh",
        "vh",
        scratch=[plane, plane, near_w_scratch, last_pair, sems, sems, sem, sem],
        flops=2 * 10**9,
    )(named, second, seeds, rinv, near_w)
    (out,) = call(
        last_body,
        "last",
        [((C, ROWS), BF16)],
        "vvvvvhv",
        "h",
        scratch=[far_scratch, last_pair, pltpu.VMEM((C, ROWS), BF16), sem, sems],
    )(recv, place, next_head, w, low, high, rinv)
    return jnp.transpose(out)


def solution(mesh):
    both = ("group", "node")
    in_specs = (P(both, None), P(None, both), P(both), P(both, None), P(both, None), P(both, None), P(both))
    return jax.shard_map(
        local, mesh=mesh, in_specs=in_specs, out_specs=P(both, None), check_vma=False
    )
```

```python
import jax
import jax.numpy as jnp
from jax import lax
from jax.experimental import pallas as pl
from jax.experimental.pallas import tpu as pltpu
from jax.sharding import PartitionSpec as P

D = 512
C = 1000
CP = 1024
BLK = 128
ROWS = 1024
TILES = ROWS // BLK
GROUPS = 16
EXT = ROWS + BLK
PAIR = 2 * BLK
PAIRS = ROWS // PAIR
SCORE_DEEP = 24
LOW = ROWS - PAIR
WEIGHT_DEEP = 16 * TILES

alpha_mix = 0.8
eps_norm = 1e-06

F32 = jnp.float32
BF16 = jnp.bfloat16
VM = pl.BlockSpec(memory_space=pltpu.VMEM)
SM = pl.BlockSpec(memory_space=pltpu.SMEM)
HB = pl.BlockSpec(memory_space=pltpu.HBM)
SPECS = {"v": VM, "s": SM, "h": HB}
NN = (((1,), (0,)), ((), ()))
NT = (((1,), (1,)), ((), ()))
TN = (((0,), (0,)), ((), ()))


def dot(a, b, dims=NN):
    return lax.dot_general(a, b, dims, preferred_element_type=F32)


def iota(shape, dim):
    return lax.broadcasted_iota(jnp.int32, shape, dim)


def call(body, name, outs, ins, out_kinds=None, scratch=(), flops=10**9, nbytes=10**6, limit=44):
    out_kinds = out_kinds or "v" * len(outs)
    return pl.pallas_call(
        body,
        name=name,
        out_shape=[jax.ShapeDtypeStruct(s, t) for s, t in outs],
        in_specs=[SPECS[k] for k in ins],
        out_specs=[SPECS[k] for k in out_kinds],
        scratch_shapes=list(scratch),
        cost_estimate=pl.CostEstimate(flops=flops, bytes_accessed=nbytes, transcendentals=0),
        compiler_params=pltpu.CompilerParams(vmem_limit_bytes=limit * 2**20),
    )


def started(copies):
    for copy in copies:
        copy.start()
    return copies


def arriving_pairs(pairs_any, to_ref, sems, count=PAIRS):
    return started(
        [
            pltpu.make_async_copy(
                pairs_any.at[r], to_ref.at[:, pl.ds(r * PAIR, PAIR)], sems.at[r]
            )
            for r in range(count)
        ]
    )


def leaving_pair(from_ref, pairs_any, sems, r):
    return started(
        [
            pltpu.make_async_copy(
                from_ref.at[:, pl.ds(r * PAIR, PAIR)], pairs_any.at[r], sems.at[r]
            )
        ]
    )


def index_body(group_any, row_any, wanted_ref, place_ref, group_ref, row_ref, sems):
    copies = started(
        [
            pltpu.make_async_copy(group_any, group_ref, sems.at[0]),
            pltpu.make_async_copy(row_any, row_ref, sems.at[1]),
        ]
    )
    for copy in copies:
        copy.wait()
    target = group_ref[...]
    rows = row_ref[...]
    member = (iota((GROUPS, BLK), 0) == target).astype(F32)
    before = (iota((BLK, BLK), 0) < iota((BLK, BLK), 1)).astype(BF16)
    earlier = dot(member.astype(BF16), before)
    slot = jnp.sum(earlier * member, axis=0, keepdims=True).astype(jnp.int32)
    in_slot = (iota((BLK, BLK), 0) == slot).astype(BF16)
    high = (rows >> 5).astype(F32)
    low = (rows & 31).astype(F32)
    wanted = 32.0 * dot((member * high).astype(BF16), in_slot, NT)
    wanted = wanted + dot((member * low).astype(BF16), in_slot, NT)
    wanted_ref[:, 0, :] = wanted.astype(jnp.int32)
    place_ref[0:1, :] = target
    place_ref[1:2, :] = slot


def unit_body(desc_ref, scales_ref, unit_ref, head_ref):
    columns = jnp.transpose(jnp.concatenate([scales_ref[...], scales_ref[...]], axis=0))
    parts = []
    total = None
    for k in range(D // BLK):
        x = desc_ref[:, k * BLK : (k + 1) * BLK].astype(F32) * columns[:, k : k + 1]
        parts.append(x)
        square = x * x
        total = square if total is None else total + square
    inv = lax.rsqrt(jnp.sum(total, axis=1, keepdims=True) + eps_norm)
    for k in range(D // BLK):
        out = (parts[k] * inv).astype(BF16)
        unit_ref[:, k * BLK : (k + 1) * BLK] = out
        head_ref[:, k * BLK : (k + 1) * BLK] = out[:BLK]


def asked_columns(asked_ref, rows):
    asked = jnp.broadcast_to(asked_ref[...].astype(F32), (GROUPS, rows, BLK))
    lane, row = iota((GROUPS, rows, BLK), 2), iota((GROUPS, rows, BLK), 1)
    return [
        jnp.sum(jnp.where(lane == slot, asked, 0.0), axis=2, keepdims=True)
        for slot in (row % 8, 8 + row % 4)
    ]


def request_rows(asked_ref):
    node = iota((GROUPS, 8, ROWS), 2).astype(F32)
    made = []
    for column in asked_columns(asked_ref, 8):
        made.append(jnp.where(node == column, 1.0, 0.0).astype(BF16).reshape(BLK, ROWS))
    return jnp.concatenate(made, axis=0)


def pack_rows(res, chunks, send_ref):
    first = iota((BLK, BLK), 0) % 8 < 4

    def part(start, k):
        return res[start : start + BLK, k * BLK : (k + 1) * BLK]

    def put(at, upper, lower):
        both = jnp.concatenate(
            [upper.reshape(GROUPS, 8, BLK), lower.reshape(GROUPS, 8, BLK)], axis=1
        )
        send_ref[:, at : at + 16, :] = both.astype(BF16)

    for k in range(chunks // 2):
        put(16 * k, part(0, 2 * k), part(0, 2 * k + 1))
    for m in range(chunks // 4):
        upper = jnp.where(first, part(BLK, 4 * m), part(BLK, 4 * m + 1))
        lower = jnp.where(first, part(BLK, 4 * m + 2), part(BLK, 4 * m + 3))
        put(8 * chunks + 16 * m, upper, lower)


def placers(place_ref):
    target, slot = place_ref[0:1, :], place_ref[1:2, :]
    row = iota((2 * BLK, BLK), 0)
    low, high = [], []
    for h in range(2):
        at = jnp.where(slot < 8, target * 16 + slot + 8 * h, -1)
        low.append((row == at).astype(F32).astype(BF16))
    for q in range(4):
        at = jnp.where(slot >= 8, target * 16 + slot - 8 + 4 * q, -1)
        high.append((row == at).astype(F32).astype(BF16))
    return jnp.concatenate(low, axis=1), jnp.concatenate(high, axis=1)


def received(recv_ref, at):
    return recv_ref[:, at : at + 16, :].reshape(2 * BLK, BLK)


def gather_units_body(asked_ref, unit_ref, send_ref):
    pack_rows(dot(request_rows(asked_ref), unit_ref[...]), D // BLK, send_ref)


def cube_pos(values):
    positive = jnp.maximum(values, 0.0)
    return positive * positive * positive


def near_body(named_ref, unit_ref, next_ref, w_any, after_ref, degree_ref, ext_ref, w_ref, w_sem):
    ext_ref[:ROWS, :] = unit_ref[...]
    ext_ref[ROWS:, :] = next_ref[...]
    for r in range(TILES):
        own = ext_ref[r * BLK : (r + 1) * BLK, :]
        w = cube_pos(dot(own, own, NT))
        degree = jnp.sum(w, axis=0, keepdims=True)
        w_ref[r, :BLK, :] = w.astype(BF16)
        after = jnp.zeros((BLK, BLK), F32)
        for k in range(2):
            tile = named_ref[r, k]
            start = pl.multiple_of(tile * BLK, BLK)
            w = cube_pos(dot(ext_ref[pl.ds(start, BLK), :], own, NT))
            degree = degree + jnp.sum(w, axis=0, keepdims=True)
            w = w.astype(BF16).astype(F32)
            inside = (tile < TILES).astype(F32)
            after = after + w * (1.0 - inside)
            w_ref[r, (k + 1) * BLK : (k + 2) * BLK, :] = (w * inside).astype(BF16)
        after_ref[:, r * BLK : (r + 1) * BLK] = after.astype(BF16)
        degree_ref[r : r + 1, :] = degree
    w_copy = pltpu.make_async_copy(w_ref, w_any.at[pl.ds(0, TILES)], w_sem)
    w_copy.start()
    w_copy.wait()


def seed_body(
    asked_ref, labels_ref, prior_any, send_ref, head_ref, seed_any,
    prior_ref, seed_ref, in_sems, sems,
):
    arriving = []
    for r in range(PAIRS):
        at = pl.ds(r * PAIR, PAIR)
        arriving += started(
            [pltpu.make_async_copy(prior_any.at[:, at], prior_ref.at[:, at], in_sems.at[r])]
        )
    rows = request_rows(asked_ref)
    seed_ref[CP - 32 :, :] = jnp.zeros((32, ROWS), BF16)
    leaving = []
    for r in range(PAIRS):
        cols = slice(r * PAIR, (r + 1) * PAIR)
        labels = labels_ref[:, cols]
        arriving[r].wait()
        hot = jnp.where(iota((C, PAIR), 0) == labels, 1.0, 0.0)
        seed = jnp.where(labels >= 0, hot, prior_ref[:, cols].astype(F32))
        seed_ref[:C, cols] = seed.astype(BF16)
        leaving += leaving_pair(seed_ref, seed_any, sems, r)
    head_ref[...] = seed_ref[:, :BLK]
    pack_rows(dot(rows, seed_ref[...], NT), CP // BLK, send_ref)
    for copy in leaving:
        copy.wait()


def degree_body(
    recv_ref, place_ref, asked_ref, unit_ref, near_ref, after_ref, asked_seed_ref, seed_ref,
    w_ref, rinv_ref, head_ref, send_ref, far_ref,
):
    w_ref[BLK:, :] = after_ref[...]
    low, high = placers(place_ref)
    for m in range(D // (4 * BLK)):
        deep = dot(high, received(recv_ref, 8 * D // BLK + 16 * m), TN)
        for j in range(2):
            flat = dot(low, received(recv_ref, 16 * (2 * m + j)), TN)
            for h in range(2):
                k = 4 * m + 2 * j + h
                part = flat[h * BLK : (h + 1) * BLK] + deep[(2 * j + h) * BLK :][:BLK]
                far_ref[:, k * BLK : (k + 1) * BLK] = part.astype(BF16)
    far = far_ref[...]
    columns = asked_columns(asked_ref, 16)
    node = iota((GROUPS, 16, BLK), 2).astype(F32)
    found = [jnp.zeros((GROUPS, 16, BLK), F32) for _ in columns]
    for r in range(TILES):
        cols = slice(r * BLK, (r + 1) * BLK)
        w = cube_pos(dot(far, unit_ref[cols, :], NT))
        w_ref[:BLK, cols] = w.astype(BF16)
        degree = near_ref[r : r + 1, :] + jnp.sum(w, axis=0, keepdims=True)
        rinv = lax.rsqrt(degree)
        rinv_ref[0:1, cols] = rinv
        if r == 0:
            head_ref[...] = (rinv * seed_ref[...].astype(F32)).astype(BF16)
        spread = jnp.broadcast_to(rinv.reshape(1, 1, BLK), (GROUPS, 16, BLK))
        for k, column in enumerate(columns):
            found[k] = jnp.where(node + float(r * BLK) == column, spread, found[k])
    weights = [jnp.sum(values, axis=2, keepdims=True) for values in found]
    for k in range(6):
        part = asked_seed_ref[:, 16 * k : 16 * (k + 1), :].astype(F32)
        send_ref[:, 16 * k : 16 * (k + 1), :] = (weights[k // 4] * part).astype(BF16)


def spread_near(named_ref, source_ref, w_ref, r):
    sources = [source_ref[:, r * BLK : (r + 1) * BLK]]
    for k in range(2):
        start = pl.multiple_of(lax.rem(named_ref[r, k], TILES) * BLK, BLK)
        sources.append(source_ref[:, pl.ds(start, BLK)])
    return dot(jnp.concatenate(sources, axis=1), w_ref[r])


def mixed_near(total, weight, seed):
    return (alpha_mix * weight) * total + (1.0 - alpha_mix) * seed.astype(F32)


def put_base(total, r, low_ref, high_ref):
    if r * BLK < LOW:
        low_ref[:, r * BLK : (r + 1) * BLK] = total.astype(BF16)
    else:
        high_ref[:, r * BLK - LOW : (r + 1) * BLK - LOW] = total.astype(BF16)


def near_first_body(
    named_ref, seed_any, rinv_ref, w_any, low_ref, high_any,
    seed_ref, first_ref, w_ref, high_ref, sems, w_sem, high_sem,
):
    w_copy = pltpu.make_async_copy(w_any.at[pl.ds(0, TILES)], w_ref, w_sem)
    w_copy.start()
    arriving = arriving_pairs(seed_any, seed_ref, sems)
    for r in range(PAIRS):
        arriving[r].wait()
        cols = slice(r * PAIR, (r + 1) * PAIR)
        first_ref[:, cols] = (rinv_ref[0:1, cols] * seed_ref[:, cols].astype(F32)).astype(BF16)
    w_copy.wait()
    for r in range(TILES):
        cols = slice(r * BLK, (r + 1) * BLK)
        weight = rinv_ref[0:1, cols]
        total = spread_near(named_ref, first_ref, w_ref, r)
        put_base(weight * mixed_near(total, weight, seed_ref[:, cols]), r, low_ref, high_ref)
    copy = pltpu.make_async_copy(high_ref, high_any.at[0], high_sem)
    copy.start()
    copy.wait()


def near_second_body(
    named_ref, second_any, seed_any, rinv_ref, w_any, low_ref, high_any,
    second_ref, seed_ref, w_ref, high_ref, sems, seed_sems, w_sem, high_sem,
):
    arriving = arriving_pairs(second_any, second_ref, sems)
    arriving += started([pltpu.make_async_copy(w_any.at[pl.ds(0, TILES)], w_ref, w_sem)])
    seeds = arriving_pairs(seed_any, seed_ref, seed_sems)
    for copy in arriving:
        copy.wait()
    for r in range(TILES):
        cols = slice(r * BLK, (r + 1) * BLK)
        total = spread_near(named_ref, second_ref, w_ref, r)
        if r % 2 == 0:
            seeds[r // 2].wait()
        put_base(mixed_near(total, rinv_ref[0:1, cols], seed_ref[:, cols]), r, low_ref, high_ref)
    copy = pltpu.make_async_copy(high_ref, high_any.at[0], high_sem)
    copy.start()
    copy.wait()


def far_scores(recv_ref, place_ref, next_ref, far_ref):
    low, high = placers(place_ref)
    for m in range(CP // (4 * BLK)):
        deep = dot(received(recv_ref, 8 * CP // BLK + 16 * m), high, TN)
        for j in range(2):
            flat = dot(received(recv_ref, 16 * (2 * m + j)), low, TN)
            for h in range(2):
                k = 4 * m + 2 * j + h
                part = flat[:, h * BLK : (h + 1) * BLK]
                part = part + deep[:, (2 * j + h) * BLK : (2 * j + h + 1) * BLK]
                far_ref[k * BLK : (k + 1) * BLK, :BLK] = part.astype(BF16)
    far_ref[:, BLK:] = next_ref[...]


def second_body(
    recv_ref, place_ref, asked_ref, next_ref, w_ref, low_ref, high_any, rinv_ref,
    second_any, head_ref, send_ref, far_ref, high_ref, second_ref, high_sem, sems,
):
    arriving = pltpu.make_async_copy(high_any.at[0], high_ref, high_sem)
    arriving.start()
    far_scores(recv_ref, place_ref, next_ref, far_ref)
    leaving = []
    for r in range(PAIRS):
        cols = slice(r * PAIR, (r + 1) * PAIR)
        total = dot(far_ref[...], w_ref[:, cols])
        weight = rinv_ref[0:1, cols]
        if r == PAIRS - 1:
            arriving.wait()
        base = low_ref[:, cols] if r < PAIRS - 1 else high_ref[...]
        total = base.astype(F32) + (alpha_mix * weight * weight) * total
        second_ref[:, cols] = total.astype(BF16)
        leaving += leaving_pair(second_ref, second_any, sems, r)
    head_ref[...] = second_ref[:, :BLK]
    pack_rows(dot(request_rows(asked_ref), second_ref[...], NT), CP // BLK, send_ref)
    for copy in leaving:
        copy.wait()


def last_body(
    recv_ref, place_ref, next_ref, w_ref, low_ref, high_any, rinv_ref,
    out_any, far_ref, high_ref, out_ref, high_sem, sems,
):
    arriving = pltpu.make_async_copy(high_any.at[0], high_ref, high_sem)
    arriving.start()
    far_scores(recv_ref, place_ref, next_ref, far_ref)
    leaving = []
    for r in range(PAIRS):
        cols = slice(r * PAIR, (r + 1) * PAIR)
        total = dot(far_ref[:C, :], w_ref[:, cols])
        if r == PAIRS - 1:
            arriving.wait()
        base = low_ref[:C, cols] if r < PAIRS - 1 else high_ref[:C, :]
        total = base.astype(F32) + (alpha_mix * rinv_ref[0:1, cols]) * total
        out_ref[:, cols] = total.astype(BF16)
        at = pl.ds(r * PAIR, PAIR)
        leaving += started(
            [pltpu.make_async_copy(out_ref.at[:, at], out_any.at[:, at], sems.at[r])]
        )
    for copy in leaving:
        copy.wait()


def passed_back(block):
    size = lax.axis_size("node")
    return lax.ppermute(block, "node", [(i, i - 1) for i in range(1, size)])


def exchanged(block):
    return lax.all_to_all(block, "group", split_axis=0, concat_axis=0, tiled=True)


def local(desc, scales, labels, prior, block_cols, cross_group, cross_row):
    named = block_cols - lax.axis_index("node") * TILES
    sem = pltpu.SemaphoreType.DMA
    sems = pltpu.SemaphoreType.DMA((PAIRS,))
    row_vector = pltpu.VMEM((1, BLK), jnp.int32)
    plane = pltpu.VMEM((CP, ROWS), BF16)
    far_scratch = pltpu.VMEM((CP, 2 * BLK), BF16)
    last_pair = pltpu.VMEM((CP, PAIR), BF16)
    base_shapes = [((CP, LOW), BF16), ((SCORE_DEEP, CP, PAIR), BF16)]
    near_w_scratch = pltpu.VMEM((TILES, 3 * BLK, BLK), BF16)
    wanted, place = call(
        index_body,
        "index",
        [((GROUPS, 1, BLK), jnp.int32), ((8, BLK), jnp.int32)],
        "hh",
        scratch=[row_vector, row_vector, pltpu.SemaphoreType.DMA((2,))],
        limit=60,
    )(cross_group.reshape(1, BLK), cross_row.reshape(1, BLK))
    asked = exchanged(wanted)
    units, head = call(
        unit_body, "units", [((ROWS, D), BF16), ((BLK, D), BF16)], "vv", nbytes=4 * 10**6
    )(desc, scales)
    next_units = passed_back(head)
    (send,) = call(gather_units_body, "gather_units", [((GROUPS, 48, BLK), BF16)], "vv")(asked, units)
    far_units = exchanged(send)
    near_w, after_w, near_degree = call(
        near_body,
        "near",
        [((WEIGHT_DEEP, 3 * BLK, BLK), BF16), ((BLK, ROWS), BF16), ((TILES, BLK), F32)],
        "svv",
        "hvv",
        scratch=[pltpu.VMEM((EXT, D), BF16), near_w_scratch, sem],
    )(named, units, next_units)
    wide_shape = ((SCORE_DEEP, CP, PAIR), BF16)
    head_shape, send_shape = ((CP, BLK), BF16), ((GROUPS, 96, BLK), BF16)
    asked_seeds, seed_head, seeds = call(
        seed_body,
        "seeds",
        [send_shape, head_shape, wide_shape],
        "vvh",
        "vvh",
        scratch=[pltpu.VMEM((C, ROWS), BF16), plane, sems, sems],
        flops=2 * 10**9,
        limit=53,
    )(asked, labels.reshape(1, ROWS), jnp.transpose(prior))
    w, rinv, head, send = call(
        degree_body,
        "degree",
        [((2 * BLK, ROWS), BF16), ((1, ROWS), F32), head_shape, send_shape],
        "vvvvvvvv",
        scratch=[pltpu.VMEM((BLK, D), BF16)],
        limit=50,
    )(far_units, place, asked, units, near_degree, after_w, asked_seeds, seed_head)
    recv = exchanged(send)
    next_head = passed_back(head)
    low, high = call(
        near_first_body,
        "near_first",
        base_shapes,
        "shvh",
        "vh",
        scratch=[plane, plane, near_w_scratch, last_pair, sems, sem, sem],
        flops=2 * 10**9,
    )(named, seeds, rinv, near_w)
    second, head, send = call(
        second_body,
        "second",
        [wide_shape, head_shape, send_shape],
        "vvvvvvhv",
        "hvv",
        scratch=[far_scratch, last_pair, plane, sem, sems],
        limit=50,
    )(recv, place, asked, next_head, w, low, high, rinv)
    recv = exchanged(send)
    next_head = passed_back(head)
    low, high = call(
        near_second_body,
        "near_second",
        base_shapes,
        "shhvh",
        "vh",
        scratch=[plane, plane, near_w_scratch, last_pair, sems, sems, sem, sem],
        flops=2 * 10**9,
    )(named, second, seeds, rinv, near_w)
    (out,) = call(
        last_body,
        "last",
        [((C, ROWS), BF16)],
        "vvvvvhv",
        "h",
        scratch=[far_scratch, last_pair, pltpu.VMEM((C, ROWS), BF16), sem, sems],
    )(recv, place, next_head, w, low, high, rinv)
    return jnp.transpose(out)


def solution(mesh):
    both = ("group", "node")
    in_specs = (P(both, None), P(None, both), P(both), P(both, None), P(both, None), P(both, None), P(both))
    return jax.shard_map(
        local, mesh=mesh, in_specs=in_specs, out_specs=P(both, None), check_vma=False
    )
```

```python
import jax
import jax.numpy as jnp
from jax import lax
from jax.experimental import pallas as pl
from jax.experimental.pallas import tpu as pltpu
from jax.sharding import PartitionSpec as P

D = 512
C = 1000
CP = 1024
BLK = 128
ROWS = 1024
TILES = ROWS // BLK
GROUPS = 16
EXT = ROWS + BLK
PAIR = 2 * BLK
PAIRS = ROWS // PAIR
SCORE_DEEP = 24
LOW = ROWS - PAIR
WEIGHT_DEEP = 16 * TILES

alpha_mix = 0.8
eps_norm = 1e-06

F32 = jnp.float32
BF16 = jnp.bfloat16
VM = pl.BlockSpec(memory_space=pltpu.VMEM)
SM = pl.BlockSpec(memory_space=pltpu.SMEM)
HB = pl.BlockSpec(memory_space=pltpu.HBM)
SPECS = {"v": VM, "s": SM, "h": HB}
NN = (((1,), (0,)), ((), ()))
NT = (((1,), (1,)), ((), ()))
TN = (((0,), (0,)), ((), ()))


def dot(a, b, dims=NN):
    return lax.dot_general(a, b, dims, preferred_element_type=F32)


def iota(shape, dim):
    return lax.broadcasted_iota(jnp.int32, shape, dim)


def call(body, name, outs, ins, out_kinds=None, scratch=(), flops=10**9, nbytes=10**6, limit=44):
    out_kinds = out_kinds or "v" * len(outs)
    return pl.pallas_call(
        body,
        name=name,
        out_shape=[jax.ShapeDtypeStruct(s, t) for s, t in outs],
        in_specs=[SPECS[k] for k in ins],
        out_specs=[SPECS[k] for k in out_kinds],
        scratch_shapes=list(scratch),
        cost_estimate=pl.CostEstimate(flops=flops, bytes_accessed=nbytes, transcendentals=0),
        compiler_params=pltpu.CompilerParams(vmem_limit_bytes=limit * 2**20),
    )


def started(copies):
    for copy in copies:
        copy.start()
    return copies


def arriving_pairs(pairs_any, to_ref, sems, count=PAIRS):
    return started(
        [
            pltpu.make_async_copy(
                pairs_any.at[r], to_ref.at[:, pl.ds(r * PAIR, PAIR)], sems.at[r]
            )
            for r in range(count)
        ]
    )


def leaving_pair(from_ref, pairs_any, sems, r):
    return started(
        [
            pltpu.make_async_copy(
                from_ref.at[:, pl.ds(r * PAIR, PAIR)], pairs_any.at[r], sems.at[r]
            )
        ]
    )


def index_body(group_any, row_any, wanted_ref, place_ref, group_ref, row_ref, sems):
    copies = started(
        [
            pltpu.make_async_copy(group_any, group_ref, sems.at[0]),
            pltpu.make_async_copy(row_any, row_ref, sems.at[1]),
        ]
    )
    for copy in copies:
        copy.wait()
    target = group_ref[...]
    rows = row_ref[...]
    member = (iota((GROUPS, BLK), 0) == target).astype(F32)
    before = (iota((BLK, BLK), 0) < iota((BLK, BLK), 1)).astype(BF16)
    earlier = dot(member.astype(BF16), before)
    slot = jnp.sum(earlier * member, axis=0, keepdims=True).astype(jnp.int32)
    in_slot = (iota((BLK, BLK), 0) == slot).astype(BF16)
    high = (rows >> 5).astype(F32)
    low = (rows & 31).astype(F32)
    wanted = 32.0 * dot((member * high).astype(BF16), in_slot, NT)
    wanted = wanted + dot((member * low).astype(BF16), in_slot, NT)
    wanted_ref[:, 0, :] = wanted.astype(jnp.int32)
    place_ref[0:1, :] = target
    place_ref[1:2, :] = slot


def unit_body(desc_ref, scales_ref, unit_ref, head_ref):
    columns = jnp.transpose(jnp.concatenate([scales_ref[...], scales_ref[...]], axis=0))
    parts = []
    total = None
    for k in range(D // BLK):
        x = desc_ref[:, k * BLK : (k + 1) * BLK].astype(F32) * columns[:, k : k + 1]
        parts.append(x)
        square = x * x
        total = square if total is None else total + square
    inv = lax.rsqrt(jnp.sum(total, axis=1, keepdims=True) + eps_norm)
    for k in range(D // BLK):
        out = (parts[k] * inv).astype(BF16)
        unit_ref[:, k * BLK : (k + 1) * BLK] = out
        head_ref[:, k * BLK : (k + 1) * BLK] = out[:BLK]


def asked_columns(asked_ref, rows):
    asked = jnp.broadcast_to(asked_ref[...].astype(F32), (GROUPS, rows, BLK))
    lane, row = iota((GROUPS, rows, BLK), 2), iota((GROUPS, rows, BLK), 1)
    return [
        jnp.sum(jnp.where(lane == slot, asked, 0.0), axis=2, keepdims=True)
        for slot in (row % 8, 8 + row % 4)
    ]


def request_rows(asked_ref):
    node = iota((GROUPS, 8, ROWS), 2).astype(F32)
    made = []
    for column in asked_columns(asked_ref, 8):
        made.append(jnp.where(node == column, 1.0, 0.0).astype(BF16).reshape(BLK, ROWS))
    return jnp.concatenate(made, axis=0)


def pack_rows(res, chunks, send_ref):
    first = iota((BLK, BLK), 0) % 8 < 4

    def part(start, k):
        return res[start : start + BLK, k * BLK : (k + 1) * BLK]

    def put(at, upper, lower):
        both = jnp.concatenate(
            [upper.reshape(GROUPS, 8, BLK), lower.reshape(GROUPS, 8, BLK)], axis=1
        )
        send_ref[:, at : at + 16, :] = both.astype(BF16)

    for k in range(chunks // 2):
        put(16 * k, part(0, 2 * k), part(0, 2 * k + 1))
    for m in range(chunks // 4):
        upper = jnp.where(first, part(BLK, 4 * m), part(BLK, 4 * m + 1))
        lower = jnp.where(first, part(BLK, 4 * m + 2), part(BLK, 4 * m + 3))
        put(8 * chunks + 16 * m, upper, lower)


def placers(place_ref):
    target, slot = place_ref[0:1, :], place_ref[1:2, :]
    row = iota((2 * BLK, BLK), 0)
    low, high = [], []
    for h in range(2):
        at = jnp.where(slot < 8, target * 16 + slot + 8 * h, -1)
        low.append((row == at).astype(F32).astype(BF16))
    for q in range(4):
        at = jnp.where(slot >= 8, target * 16 + slot - 8 + 4 * q, -1)
        high.append((row == at).astype(F32).astype(BF16))
    return jnp.concatenate(low, axis=1), jnp.concatenate(high, axis=1)


def received(recv_ref, at):
    return recv_ref[:, at : at + 16, :].reshape(2 * BLK, BLK)


def gather_units_body(asked_ref, unit_ref, send_ref):
    pack_rows(dot(request_rows(asked_ref), unit_ref[...]), D // BLK, send_ref)


def cube_pos(values):
    positive = jnp.maximum(values, 0.0)
    return positive * positive * positive


def near_body(named_ref, unit_ref, next_ref, w_any, after_ref, degree_ref, ext_ref, w_ref, w_sem):
    ext_ref[:ROWS, :] = unit_ref[...]
    ext_ref[ROWS:, :] = next_ref[...]
    for r in range(TILES):
        own = ext_ref[r * BLK : (r + 1) * BLK, :]
        w = cube_pos(dot(own, own, NT))
        degree = jnp.sum(w, axis=0, keepdims=True)
        w_ref[r, :BLK, :] = w.astype(BF16)
        after = jnp.zeros((BLK, BLK), F32)
        for k in range(2):
            tile = named_ref[k, r]
            start = pl.multiple_of(tile * BLK, BLK)
            w = cube_pos(dot(ext_ref[pl.ds(start, BLK), :], own, NT))
            degree = degree + jnp.sum(w, axis=0, keepdims=True)
            w = w.astype(BF16).astype(F32)
            inside = (tile < TILES).astype(F32)
            after = after + w * (1.0 - inside)
            w_ref[r, (k + 1) * BLK : (k + 2) * BLK, :] = (w * inside).astype(BF16)
        after_ref[:, r * BLK : (r + 1) * BLK] = after.astype(BF16)
        degree_ref[r : r + 1, :] = degree
    w_copy = pltpu.make_async_copy(w_ref, w_any.at[pl.ds(0, TILES)], w_sem)
    w_copy.start()
    w_copy.wait()


def seed_body(
    asked_ref, labels_ref, prior_any, send_ref, head_ref, seed_any,
    prior_ref, seed_ref, in_sems, sems,
):
    arriving = []
    for r in range(PAIRS):
        at = pl.ds(r * PAIR, PAIR)
        arriving += started(
            [pltpu.make_async_copy(prior_any.at[:, at], prior_ref.at[:, at], in_sems.at[r])]
        )
    rows = request_rows(asked_ref)
    seed_ref[CP - 32 :, :] = jnp.zeros((32, ROWS), BF16)
    leaving = []
    for r in range(PAIRS):
        cols = slice(r * PAIR, (r + 1) * PAIR)
        labels = labels_ref[:, cols]
        arriving[r].wait()
        hot = jnp.where(iota((C, PAIR), 0) == labels, 1.0, 0.0)
        seed = jnp.where(labels >= 0, hot, prior_ref[:, cols].astype(F32))
        seed_ref[:C, cols] = seed.astype(BF16)
        leaving += leaving_pair(seed_ref, seed_any, sems, r)
    head_ref[...] = seed_ref[:, :BLK]
    pack_rows(dot(rows, seed_ref[...], NT), CP // BLK, send_ref)
    for copy in leaving:
        copy.wait()


def degree_body(
    recv_ref, place_ref, asked_ref, unit_ref, near_ref, after_ref, asked_seed_ref, seed_ref,
    w_ref, rinv_ref, head_ref, send_ref, far_ref,
):
    w_ref[BLK:, :] = after_ref[...]
    low, high = placers(place_ref)
    for m in range(D // (4 * BLK)):
        deep = dot(high, received(recv_ref, 8 * D // BLK + 16 * m), TN)
        for j in range(2):
            flat = dot(low, received(recv_ref, 16 * (2 * m + j)), TN)
            for h in range(2):
                k = 4 * m + 2 * j + h
                part = flat[h * BLK : (h + 1) * BLK] + deep[(2 * j + h) * BLK :][:BLK]
                far_ref[:, k * BLK : (k + 1) * BLK] = part.astype(BF16)
    far = far_ref[...]
    columns = asked_columns(asked_ref, 16)
    node = iota((GROUPS, 16, BLK), 2).astype(F32)
    found = [jnp.zeros((GROUPS, 16, BLK), F32) for _ in columns]
    for r in range(TILES):
        cols = slice(r * BLK, (r + 1) * BLK)
        w = cube_pos(dot(far, unit_ref[cols, :], NT))
        w_ref[:BLK, cols] = w.astype(BF16)
        degree = near_ref[r : r + 1, :] + jnp.sum(w, axis=0, keepdims=True)
        rinv = lax.rsqrt(degree)
        rinv_ref[0:1, cols] = rinv
        if r == 0:
            head_ref[...] = (rinv * seed_ref[...].astype(F32)).astype(BF16)
        spread = jnp.broadcast_to(rinv.reshape(1, 1, BLK), (GROUPS, 16, BLK))
        for k, column in enumerate(columns):
            found[k] = jnp.where(node + float(r * BLK) == column, spread, found[k])
    weights = [jnp.sum(values, axis=2, keepdims=True) for values in found]
    for k in range(6):
        part = asked_seed_ref[:, 16 * k : 16 * (k + 1), :].astype(F32)
        send_ref[:, 16 * k : 16 * (k + 1), :] = (weights[k // 4] * part).astype(BF16)


def spread_near(named_ref, source_ref, w_ref, r):
    sources = [source_ref[:, r * BLK : (r + 1) * BLK]]
    for k in range(2):
        start = pl.multiple_of(lax.rem(named_ref[k, r], TILES) * BLK, BLK)
        sources.append(source_ref[:, pl.ds(start, BLK)])
    return dot(jnp.concatenate(sources, axis=1), w_ref[r])


def mixed_near(total, weight, seed):
    return (alpha_mix * weight) * total + (1.0 - alpha_mix) * seed.astype(F32)


def put_base(total, r, low_ref, high_ref):
    if r * BLK < LOW:
        low_ref[:, r * BLK : (r + 1) * BLK] = total.astype(BF16)
    else:
        high_ref[:, r * BLK - LOW : (r + 1) * BLK - LOW] = total.astype(BF16)


def near_first_body(
    named_ref, seed_any, rinv_ref, w_any, low_ref, high_any,
    seed_ref, first_ref, w_ref, high_ref, sems, w_sem, high_sem,
):
    w_copy = pltpu.make_async_copy(w_any.at[pl.ds(0, TILES)], w_ref, w_sem)
    w_copy.start()
    arriving = arriving_pairs(seed_any, seed_ref, sems)
    for r in range(PAIRS):
        arriving[r].wait()
        cols = slice(r * PAIR, (r + 1) * PAIR)
        first_ref[:, cols] = (rinv_ref[0:1, cols] * seed_ref[:, cols].astype(F32)).astype(BF16)
    w_copy.wait()
    for r in range(TILES):
        cols = slice(r * BLK, (r + 1) * BLK)
        weight = rinv_ref[0:1, cols]
        total = spread_near(named_ref, first_ref, w_ref, r)
        put_base(weight * mixed_near(total, weight, seed_ref[:, cols]), r, low_ref, high_ref)
    copy = pltpu.make_async_copy(high_ref, high_any.at[0], high_sem)
    copy.start()
    copy.wait()


def near_second_body(
    named_ref, second_any, seed_any, rinv_ref, w_any, low_ref, high_any,
    second_ref, seed_ref, w_ref, high_ref, sems, seed_sems, w_sem, high_sem,
):
    arriving = arriving_pairs(second_any, second_ref, sems)
    arriving += started([pltpu.make_async_copy(w_any.at[pl.ds(0, TILES)], w_ref, w_sem)])
    seeds = arriving_pairs(seed_any, seed_ref, seed_sems)
    for copy in arriving:
        copy.wait()
    for r in range(TILES):
        cols = slice(r * BLK, (r + 1) * BLK)
        total = spread_near(named_ref, second_ref, w_ref, r)
        if r % 2 == 0:
            seeds[r // 2].wait()
        put_base(mixed_near(total, rinv_ref[0:1, cols], seed_ref[:, cols]), r, low_ref, high_ref)
    copy = pltpu.make_async_copy(high_ref, high_any.at[0], high_sem)
    copy.start()
    copy.wait()


def far_scores(recv_ref, place_ref, next_ref, far_ref):
    low, high = placers(place_ref)
    for m in range(CP // (4 * BLK)):
        deep = dot(received(recv_ref, 8 * CP // BLK + 16 * m), high, TN)
        for j in range(2):
            flat = dot(received(recv_ref, 16 * (2 * m + j)), low, TN)
            for h in range(2):
                k = 4 * m + 2 * j + h
                part = flat[:, h * BLK : (h + 1) * BLK]
                part = part + deep[:, (2 * j + h) * BLK : (2 * j + h + 1) * BLK]
                far_ref[k * BLK : (k + 1) * BLK, :BLK] = part.astype(BF16)
    far_ref[:, BLK:] = next_ref[...]


def second_body(
    recv_ref, place_ref, asked_ref, next_ref, w_ref, low_ref, high_any, rinv_ref,
    second_any, head_ref, send_ref, far_ref, high_ref, second_ref, high_sem, sems,
):
    arriving = pltpu.make_async_copy(high_any.at[0], high_ref, high_sem)
    arriving.start()
    far_scores(recv_ref, place_ref, next_ref, far_ref)
    leaving = []
    for r in range(PAIRS):
        cols = slice(r * PAIR, (r + 1) * PAIR)
        total = dot(far_ref[...], w_ref[:, cols])
        weight = rinv_ref[0:1, cols]
        if r == PAIRS - 1:
            arriving.wait()
        base = low_ref[:, cols] if r < PAIRS - 1 else high_ref[...]
        total = base.astype(F32) + (alpha_mix * weight * weight) * total
        second_ref[:, cols] = total.astype(BF16)
        leaving += leaving_pair(second_ref, second_any, sems, r)
    head_ref[...] = second_ref[:, :BLK]
    pack_rows(dot(request_rows(asked_ref), second_ref[...], NT), CP // BLK, send_ref)
    for copy in leaving:
        copy.wait()


def last_body(
    recv_ref, place_ref, next_ref, w_ref, low_ref, high_any, rinv_ref,
    out_any, far_ref, high_ref, out_ref, high_sem, sems,
):
    arriving = pltpu.make_async_copy(high_any.at[0], high_ref, high_sem)
    arriving.start()
    far_scores(recv_ref, place_ref, next_ref, far_ref)
    leaving = []
    for r in range(PAIRS):
        cols = slice(r * PAIR, (r + 1) * PAIR)
        total = dot(far_ref[:C, :], w_ref[:, cols])
        if r == PAIRS - 1:
            arriving.wait()
        base = low_ref[:C, cols] if r < PAIRS - 1 else high_ref[:C, :]
        total = base.astype(F32) + (alpha_mix * rinv_ref[0:1, cols]) * total
        out_ref[:, cols] = total.astype(BF16)
        at = pl.ds(r * PAIR, PAIR)
        leaving += started(
            [pltpu.make_async_copy(out_ref.at[:, at], out_any.at[:, at], sems.at[r])]
        )
    for copy in leaving:
        copy.wait()


def passed_back(block):
    size = lax.axis_size("node")
    return lax.ppermute(block, "node", [(i, i - 1) for i in range(1, size)])


def exchanged(block):
    return lax.all_to_all(block, "group", split_axis=0, concat_axis=0, tiled=True)


def local(desc, scales, labels, prior, block_cols, cross_group, cross_row):
    named = jnp.transpose(block_cols) - lax.axis_index("node") * TILES
    sem = pltpu.SemaphoreType.DMA
    sems = pltpu.SemaphoreType.DMA((PAIRS,))
    row_vector = pltpu.VMEM((1, BLK), jnp.int32)
    plane = pltpu.VMEM((CP, ROWS), BF16)
    far_scratch = pltpu.VMEM((CP, 2 * BLK), BF16)
    last_pair = pltpu.VMEM((CP, PAIR), BF16)
    base_shapes = [((CP, LOW), BF16), ((SCORE_DEEP, CP, PAIR), BF16)]
    near_w_scratch = pltpu.VMEM((TILES, 3 * BLK, BLK), BF16)
    wanted, place = call(
        index_body,
        "index",
        [((GROUPS, 1, BLK), jnp.int32), ((8, BLK), jnp.int32)],
        "hh",
        scratch=[row_vector, row_vector, pltpu.SemaphoreType.DMA((2,))],
        limit=60,
    )(cross_group.reshape(1, BLK), cross_row.reshape(1, BLK))
    asked = exchanged(wanted)
    units, head = call(
        unit_body, "units", [((ROWS, D), BF16), ((BLK, D), BF16)], "vv", nbytes=4 * 10**6
    )(desc, scales)
    next_units = passed_back(head)
    (send,) = call(gather_units_body, "gather_units", [((GROUPS, 48, BLK), BF16)], "vv")(asked, units)
    far_units = exchanged(send)
    near_w, after_w, near_degree = call(
        near_body,
        "near",
        [((WEIGHT_DEEP, 3 * BLK, BLK), BF16), ((BLK, ROWS), BF16), ((TILES, BLK), F32)],
        "svv",
        "hvv",
        scratch=[pltpu.VMEM((EXT, D), BF16), near_w_scratch, sem],
    )(named, units, next_units)
    wide_shape = ((SCORE_DEEP, CP, PAIR), BF16)
    head_shape, send_shape = ((CP, BLK), BF16), ((GROUPS, 96, BLK), BF16)
    asked_seeds, seed_head, seeds = call(
        seed_body,
        "seeds",
        [send_shape, head_shape, wide_shape],
        "vvh",
        "vvh",
        scratch=[pltpu.VMEM((C, ROWS), BF16), plane, sems, sems],
        flops=2 * 10**9,
        limit=53,
    )(asked, labels.reshape(1, ROWS), jnp.transpose(prior))
    w, rinv, head, send = call(
        degree_body,
        "degree",
        [((2 * BLK, ROWS), BF16), ((1, ROWS), F32), head_shape, send_shape],
        "vvvvvvvv",
        scratch=[pltpu.VMEM((BLK, D), BF16)],
        limit=50,
    )(far_units, place, asked, units, near_degree, after_w, asked_seeds, seed_head)
    recv = exchanged(send)
    next_head = passed_back(head)
    low, high = call(
        near_first_body,
        "near_first",
        base_shapes,
        "shvh",
        "vh",
        scratch=[plane, plane, near_w_scratch, last_pair, sems, sem, sem],
        flops=2 * 10**9,
    )(named, seeds, rinv, near_w)
    second, head, send = call(
        second_body,
        "second",
        [wide_shape, head_shape, send_shape],
        "vvvvvvhv",
        "hvv",
        scratch=[far_scratch, last_pair, plane, sem, sems],
        limit=50,
    )(recv, place, asked, next_head, w, low, high, rinv)
    recv = exchanged(send)
    next_head = passed_back(head)
    low, high = call(
        near_second_body,
        "near_second",
        base_shapes,
        "shhvh",
        "vh",
        scratch=[plane, plane, near_w_scratch, last_pair, sems, sems, sem, sem],
        flops=2 * 10**9,
    )(named, second, seeds, rinv, near_w)
    (out,) = call(
        last_body,
        "last",
        [((C, ROWS), BF16)],
        "vvvvvhv",
        "h",
        scratch=[far_scratch, last_pair, pltpu.VMEM((C, ROWS), BF16), sem, sems],
    )(recv, place, next_head, w, low, high, rinv)
    return jnp.transpose(out)


def solution(mesh):
    both = ("group", "node")
    in_specs = (P(both, None), P(None, both), P(both), P(both, None), P(both, None), P(both, None), P(both))
    return jax.shard_map(
        local, mesh=mesh, in_specs=in_specs, out_specs=P(both, None), check_vma=False
    )
```
